256 devices in a mesh: stream: 4 (over x), expert: 64 (over y, z, core).
Axes of the slice: x: 4, y: 4, z: 8, core: 2. Of those that a mesh axis runs over, the one named last changes fastest.
Arguments:
- streams: bfloat16 [8192, 4, 7168], P('expert', 'stream'), may hold values from -350 to 350
- cotangent: bfloat16 [8192, 4, 7168], P('expert', 'stream'), may hold values from -6 to 6
- moe_out: bfloat16 [8192, 7168], P('expert', 'stream'), may hold values from -6 to 6
- coef_proj: bfloat16 [4, 24, 7168], P(None, None, 'stream'), may hold values from -0.03125 to 0.03125
- coef_scale: float32 [3], replicated, may hold values from 0.5 to 1.5
- coef_bias: float32 [24], replicated, may hold values from -3 to 3
- norm_gain: bfloat16 [7168], P('stream'), may hold values from 0.099609375 to 1.8984375
- expert_ids: int32 [8192, 2], P('expert'), may hold values from 0 to 31, all different within a row; in each aligned block of 128 rows (0 to 127, 128 to 255, ...) at most 16 rows name the same one
- combine: float32 [8192, 2], P('expert'), may hold values from 0.1 to 1
- w_gate: bfloat16 [7168, 32768], P('stream', 'expert'), may hold values from -0.0625 to 0.0625
- w_up: bfloat16 [7168, 32768], P('stream', 'expert'), may hold values from -0.0625 to 0.0625
- w_down: bfloat16 [32768, 7168], P('expert', 'stream'), may hold values from -0.1875 to 0.1875
Outputs:
- d_streams: bfloat16 [8192, 4, 7168], P('expert', 'stream')
The draws below stay inside these ranges and needn't reach their ends.
Inputs may be any that keep to these rules, and one draw needn't show every extreme that they name: `expert_ids`: within each aligned block of 128 rows (the rows of one device) no expert is named more than 16 times, a bound that some block reaches.
All inputs are finite; a program needn't handle non-finite values.
Results may differ from the reference program's by a relative error of at most 0.006.
Values may be sent and summed in bfloat16 or wider, within the bound.
No kernel may reach another device: no remote copies, remote signals or barrier semaphores. Data moves between devices by JAX's collectives and lax.ppermute only.
A program may use at most 128 MiB of HBM per device.

```python
import math
import jax
import jax.numpy as jnp
import numpy as np
from jax import lax

D = 7168
NSTREAM = 4
COEF = 24
SINK = 4
FFW = 1024
TOP = 2
TOK_DEV = 128
TOKENS = 8192
EXPERTS = 32
CAP = 16
N_EXPERT = 64


def draw_streams(key, part):
    key = jax.random.fold_in(key, 11)
    first_key, row_key, col_key = jax.random.split(key, 3)
    row_scale = jnp.exp(jax.random.uniform(row_key, (TOKENS, 1, 1), jnp.float32, 0.0, math.log(10.0)))
    position = jnp.arange(D, dtype=jnp.float32) / (D - 1)
    ramp = 1.0 + 3.0 * position
    col_scale = jnp.exp(jax.random.uniform(col_key, (1, NSTREAM, D), jnp.float32, 0.0, math.log(2.5))) * ramp[None, None, :]
    base = jax.random.truncated_normal(first_key, -3.0, 3.0, (TOKENS, NSTREAM, D), jnp.float32)
    return (base * row_scale * col_scale).astype(jnp.bfloat16)


def level_of(rng, shape, cuts, smallest, top_value):
    level = 1.0
    for dim, shards_of in cuts:
        draws = jax.random.uniform(jax.random.fold_in(jax.random.fold_in(rng, 6), dim), (shards_of,), jnp.float32, smallest / len(cuts), top_value / len(cuts))
        level = level * jnp.repeat(jnp.exp(draws), shape[dim] // shards_of).reshape((-1,) + (1,) * (len(shape) - 1 - dim))
    return level


def shared_out(own_key, own, number, rows, number_of, top, most, slope):
    order = jax.random.permutation(own_key, number_of)
    heavy_load, common = shares(number_of, rows * top, most, slope, True), shares(number_of, rows * top, most, slope, False)
    places = jnp.arange(number_of)

    def named(lengths, rotation):
        used = int((lengths > 0).sum())
        fixed = max(1, used // 4)
        passed = fixed + (places - fixed + rotation * (used - fixed)) % max(1, number_of - fixed)
        return jnp.zeros((number_of,), jnp.int32).at[order[jnp.where(places < fixed, places, passed)]].set(jnp.asarray(lengths, jnp.int32))

    lengths = jnp.where(number % 4 == 0, named(heavy_load, number // 4), named(common, number - number // 4 - 1))
    mixed = jax.random.permutation(jax.random.fold_in(own, 3), number_of)
    giver, sink = mixed[0:number_of // 2 * 2:2], mixed[1:number_of // 2 * 2:2]
    room = jnp.minimum(lengths[giver] - 1, most - lengths[sink]) // 2
    room = jnp.where((giver == order[0]) | (sink == order[0]) | (lengths[sink] == 0), 0, jnp.maximum(room, 0))
    passed = jax.random.randint(jax.random.fold_in(own, 4), (number_of // 2,), 0, 1 << 20) % (room + 1)
    lengths = lengths.at[giver].add(-passed).at[sink].add(passed)
    members = jnp.searchsorted(jnp.cumsum(lengths), jnp.arange(rows * top), side="right").astype(jnp.int32)
    listing = members.reshape(top, rows).T
    listing = listing[jax.random.permutation(jax.random.fold_in(own, 1), rows)]
    rotation = jax.random.randint(jax.random.fold_in(own, 2), (rows, 1), 0, top)
    return jnp.take_along_axis(listing, (jnp.arange(top)[None, :] + rotation) % top, axis=1)


def shares(count, total, bound, skew, full):
    weights = [(1 << 20) // math.isqrt(grade ** skew) + 1 for grade in range(1, count + 1)]
    largest = bound if full else min(bound, max(-(-total // count), total * weights[0] // sum(weights)))
    least = 1 if total - largest >= count - 1 else 0
    holding, surplus = [largest] + [least] * (count - 1), total - largest - least * (count - 1)
    while surplus > 0:
        free = [i for i in range(1, count) if holding[i] < largest] or [i for i in range(1, count) if holding[i] < bound]
        whole, remaining = sum([weights[i] for i in free]), surplus
        for i in free:
            addition = min(bound - holding[i], max(1, remaining * weights[i] // whole), surplus)
            holding[i] = holding[i] + addition
            surplus = surplus - addition
    return np.array(holding)


def scatter_about(key, shape, scale, bound, cuts=(), held_as=jnp.bfloat16):
    result = scale * jax.random.normal(key, shape, jnp.float32)
    if cuts:
        result = result * level_of(key, shape, cuts, -0.22, 0.18)
    return jnp.clip(result, -bound, bound).astype(held_as)


def setup_inputs(seed: int = 0) -> dict:
    keys = jax.random.split(jax.random.key(seed), 13)
    streams = draw_streams(jax.random.fold_in(keys[12], 71), 0)
    cotangent = scatter_about(keys[1], (TOKENS, NSTREAM, D), 1.0, 6.0, ((0, 64), (1, 4)))
    moe_out = scatter_about(keys[2], (TOKENS, D), 1.0, 6.0, ((0, 64), (1, 4)))
    coef_proj = scatter_about(keys[3], (NSTREAM, COEF, D), (NSTREAM * D) ** -0.5, 0.03125, ((2, 4),))
    coef_scale = jnp.clip(jax.random.uniform(keys[4], (3,), jnp.float32, 0.5, 1.5), 0.5, 1.5)
    coef_bias = scatter_about(keys[5], (COEF,), 1.0, 3.0, (), jnp.float32)
    norm_gain = jnp.clip(1.0 + 0.18 * jax.random.normal(keys[6], (D,), jnp.float32), 0.099609375, 1.8984375).astype(jnp.bfloat16)
    expert_ids_keys = jax.random.split(jax.random.fold_in(keys[7], 1), TOKENS // TOK_DEV)
    expert_ids_turns = jax.random.permutation(jax.random.fold_in(keys[7], 3), TOKENS // TOK_DEV)
    expert_ids = jax.vmap(lambda own, number: shared_out(jax.random.fold_in(keys[7], 2), own, number, TOK_DEV, EXPERTS, TOP, CAP, 2))(expert_ids_keys, expert_ids_turns).reshape((TOKENS, TOP))
    combine = jnp.clip(0.1 + 0.9 * jax.random.uniform(keys[8], (TOKENS, TOP), jnp.float32) ** level_of(keys[8], (TOKENS, TOP), ((0, 64),), -0.2, 0.2), 0.1, 1.0)
    w_gate = scatter_about(keys[9], (D, EXPERTS * FFW), D ** -0.5, 0.0625, ((0, 4), (1, 64)))
    w_up = scatter_about(keys[10], (D, EXPERTS * FFW), D ** -0.5, 0.0625, ((0, 4), (1, 64)))
    w_down = scatter_about(keys[11], (EXPERTS * FFW, D), FFW ** -0.5, 0.1875, ((0, 64), (1, 4)))
    return dict(streams=streams, cotangent=cotangent, moe_out=moe_out, coef_proj=coef_proj, coef_scale=coef_scale, coef_bias=coef_bias, norm_gain=norm_gain, expert_ids=expert_ids, combine=combine, w_gate=w_gate, w_up=w_up, w_down=w_down)


EPSILON = 1e-06
HIGH = lax.Precision.HIGHEST

def coefficients(projection, coef_scale, coef_bias):
    pre_weights = jax.nn.sigmoid(coef_scale[0] * projection[0:NSTREAM] + coef_bias[0:NSTREAM, None])
    post_weights = 2.0 * jax.nn.sigmoid(coef_scale[1] * projection[NSTREAM:2 * NSTREAM] + coef_bias[NSTREAM:2 * NSTREAM, None])
    logits = coef_scale[2] * projection[2 * NSTREAM:] + coef_bias[2 * NSTREAM:, None]
    mixing = jnp.exp(logits).reshape(NSTREAM, NSTREAM, -1)
    for iteration in range(SINK):
        mixing = mixing / lax.optimization_barrier(jnp.sum(mixing, axis=1, keepdims=True))
        mixing = mixing / lax.optimization_barrier(jnp.sum(mixing, axis=0, keepdims=True))
    return (pre_weights, post_weights, mixing)

def recompute(x_block, dy_block, moe_block, coef_proj, coef_scale, coef_bias, norm_gain):
    x_rows = x_block.astype(jnp.float32)
    dy_rows = dy_block.astype(jnp.float32)
    moe_rows = moe_block.astype(jnp.float32)
    table = coef_proj.astype(jnp.float32)
    squares = lax.optimization_barrier(jnp.sum(x_rows * x_rows, axis=(1, 2)))
    projected = jnp.einsum('tid,icd->ct', x_rows, table, precision=HIGH)
    post_dots = jnp.einsum('tid,td->it', dy_rows, moe_rows, precision=HIGH)
    mix_dots = jnp.einsum('tid,tjd->ijt', dy_rows, x_rows, precision=HIGH)
    rscale = lax.rsqrt(squares / (NSTREAM * D) + EPSILON)
    projection = projected * rscale[None, :]
    pre_weights, post_weights, mixing = coefficients(projection, coef_scale, coef_bias)
    mixed_rows = lax.optimization_barrier(jnp.sum(pre_weights.T[:, :, None] * x_rows, axis=1))
    qscale = lax.rsqrt(lax.optimization_barrier(jnp.mean(mixed_rows * mixed_rows, axis=1)) + EPSILON)
    normed = (mixed_rows * qscale[:, None] * norm_gain.astype(jnp.float32)[None, :]).astype(jnp.bfloat16)
    d_moe = lax.optimization_barrier(jnp.sum(post_weights.T[:, :, None] * dy_rows, axis=1))
    return (x_rows, dy_rows, table, projected, rscale, projection, pre_weights, mixing, post_dots, mix_dots, mixed_rows, qscale, normed, d_moe)

def reference(streams, cotangent, moe_out, coef_proj, coef_scale, coef_bias, norm_gain, expert_ids, combine, w_gate, w_up, w_down):
    blocks = N_EXPERT
    x_blocks = streams.reshape(blocks, TOK_DEV, NSTREAM, D)
    dy_blocks = cotangent.reshape(blocks, TOK_DEV, NSTREAM, D)
    moe_blocks = moe_out.reshape(blocks, TOK_DEV, D)

    def first_pass(pieces):
        state = recompute(pieces[0], pieces[1], pieces[2], coef_proj, coef_scale, coef_bias, norm_gain)
        return (state[12], state[13])
    normed_all, dmoe_all = lax.map(first_pass, (x_blocks, dy_blocks, moe_blocks))
    normed_all = normed_all.reshape(TOKENS, D)
    dmoe_all = dmoe_all.reshape(TOKENS, D)
    ids_blocks = expert_ids.reshape(blocks, TOK_DEV, TOP)
    expert_hits = (ids_blocks[..., None] == jnp.arange(EXPERTS, dtype=jnp.int32)).astype(jnp.int32)
    per_token = lax.optimization_barrier(jnp.sum(expert_hits, axis=2))
    earlier = jnp.cumsum(per_token, axis=1) - per_token
    position = lax.optimization_barrier(jnp.sum(expert_hits * earlier[:, :, None, :], axis=3))
    source = jnp.arange(blocks, dtype=jnp.int32)[:, None, None]
    slot_flat = ((source * EXPERTS + ids_blocks) * CAP + position).reshape(-1).astype(jnp.int32)
    assignment = jnp.arange(TOKENS * TOP, dtype=jnp.int32)
    slot_table = jnp.full((blocks * EXPERTS * CAP,), TOKENS * TOP, dtype=jnp.int32).at[slot_flat].set(assignment)
    slot_table = slot_table.reshape(blocks, EXPERTS, CAP)
    slot_cot = (combine[:, :, None] * dmoe_all[:, None, :]).astype(jnp.bfloat16).reshape(TOKENS * TOP, D)
    cot_ext = jnp.concatenate([slot_cot, jnp.zeros((1, D), jnp.bfloat16)], axis=0)
    normed_ext = jnp.concatenate([normed_all, jnp.zeros((1, D), jnp.bfloat16)], axis=0)

    def expert_step(grad_acc, expert):
        slot_index = lax.dynamic_index_in_dim(slot_table, expert, 1, keepdims=False).reshape(-1)
        token_rows = slot_index // TOP
        rows_u = normed_ext[token_rows]
        rows_c = cot_ext[slot_index]
        gate_cols = lax.dynamic_slice_in_dim(w_gate, expert * FFW, FFW, 1)
        up_cols = lax.dynamic_slice_in_dim(w_up, expert * FFW, FFW, 1)
        down_rows = lax.dynamic_slice_in_dim(w_down, expert * FFW, FFW, 0)
        gate_val = jnp.dot(rows_u, gate_cols, preferred_element_type=jnp.float32)
        up_value = jnp.dot(rows_u, up_cols, preferred_element_type=jnp.float32)
        d_hidden = jnp.dot(rows_c, down_rows.T, preferred_element_type=jnp.float32)
        sigmoid_gate = jax.nn.sigmoid(gate_val)
        d_gate = (d_hidden * up_value * sigmoid_gate * (1.0 + gate_val * (1.0 - sigmoid_gate))).astype(jnp.bfloat16)
        d_up = (d_hidden * gate_val * sigmoid_gate).astype(jnp.bfloat16)
        slot_grad = jnp.dot(d_gate, gate_cols.T, preferred_element_type=jnp.float32) + jnp.dot(d_up, up_cols.T, preferred_element_type=jnp.float32)
        return (grad_acc.at[token_rows].add(slot_grad), None)
    grad_ext, _ = lax.scan(expert_step, jnp.zeros((TOKENS + 1, D), jnp.float32), jnp.arange(EXPERTS, dtype=jnp.int32))
    du_blocks = grad_ext[:TOKENS].reshape(blocks, TOK_DEV, D)

    def second_pass(pieces):
        state = recompute(pieces[0], pieces[1], pieces[2], coef_proj, coef_scale, coef_bias, norm_gain)
        x_rows, dy_rows, table, projected, rscale, projection, pre_weights, mixing, post_dots, mix_dots, mixed_rows, qscale, normed, d_moe = state
        grad_in = norm_gain.astype(jnp.float32)[None, :] * pieces[3]
        norm_dot = lax.optimization_barrier(jnp.sum(grad_in * mixed_rows, axis=1))
        a_part = jnp.einsum('td,tid->it', grad_in, x_rows, precision=HIGH)
        b_part = jnp.einsum('td,tid->it', mixed_rows, x_rows, precision=HIGH)
        cube_term = qscale ** 3 / D * norm_dot
        d_pre = qscale[None, :] * a_part - cube_term[None, :] * b_part
        d_mixed = qscale[:, None] * grad_in - mixed_rows * cube_term[:, None]
        _, pullback = jax.vjp(lambda values: coefficients(values, coef_scale, coef_bias), projection)
        d_proj, = pullback((d_pre, post_dots, mix_dots))
        d_projected = rscale[None, :] * d_proj
        d_rscale = lax.optimization_barrier(jnp.sum(d_proj * projected, axis=0))
        d_square = -0.5 * rscale ** 3 / (NSTREAM * D) * d_rscale
        grad_coef = jnp.einsum('ct,icd->tid', d_projected, table, precision=HIGH) + x_rows * (2.0 * d_square)[:, None, None]
        grad_pre = pre_weights.T[:, :, None] * d_mixed[:, None, :]
        grad_res = jnp.einsum('ijt,tid->tjd', mixing, dy_rows, precision=HIGH)
        return (grad_res + grad_pre + grad_coef).astype(jnp.bfloat16)
    grads = lax.map(second_pass, (x_blocks, dy_blocks, moe_blocks, du_blocks))
    return grads.reshape(TOKENS, NSTREAM, D)
```

```python
import jax
import jax.numpy as jnp
from jax import lax
from jax.experimental import pallas as pl
from jax.experimental.pallas import tpu as pltpu
from jax.sharding import PartitionSpec as P

D = 7168
NSTREAM = 4
SINK = 4
TOP = 2
EPSILON = 1e-06
F32 = jnp.float32
BF16 = jnp.bfloat16
ROWS = 16
LANES = 128
VMEM_LIMIT = 48 * 1024 * 1024
CONTRACT_LAST = (((1,), (1,)), ((), ()))


def sinkhorn(logits):
    mixing = jnp.exp(logits).reshape(NSTREAM, NSTREAM, -1)
    for iteration in range(SINK):
        mixing = mixing / jnp.sum(mixing, axis=1, keepdims=True)
        mixing = mixing / jnp.sum(mixing, axis=0, keepdims=True)
    return mixing


def relative(array, me, axis=0):
    flipped = jnp.flip(array, axis)
    doubled = jnp.concatenate([flipped, flipped], axis)
    return lax.dynamic_slice_in_dim(doubled, NSTREAM - 1 - me, NSTREAM, axis)


def shift(array, step):
    pairs = [(i, (i + step) % NSTREAM) for i in range(NSTREAM)]
    return lax.ppermute(array, "stream", pairs)


def small_sum(array):
    return array + shift(array, 1) + shift(array, 2) + shift(array, 3)


def spread(array):
    return [array, shift(array, 1), shift(array, 2), shift(array, 3)]


def whole(count):
    return [pl.BlockSpec(memory_space=pltpu.VMEM)] * count


def call(kernel, name, out_shape, args, scratch=(), flops=0):
    single = not isinstance(out_shape, (list, tuple))
    outs = [out_shape] if single else list(out_shape)
    moved = sum(a.size * a.dtype.itemsize for a in list(args) + outs)
    return pl.pallas_call(
        kernel,
        out_shape=out_shape,
        in_specs=whole(len(args)),
        out_specs=whole(1)[0] if single else whole(len(outs)),
        scratch_shapes=list(scratch),
        compiler_params=pltpu.CompilerParams(vmem_limit_bytes=VMEM_LIMIT),
        cost_estimate=pl.CostEstimate(flops=flops, bytes_accessed=moved, transcendentals=0),
        name=name,
    )(*args)


def sds(shape, dtype):
    return jax.ShapeDtypeStruct(shape, dtype)


def project_kernel(x0, x1, x2, x3, p0, p1, p2, p3, out_ref, stat):
    xs, ps = (x0, x1, x2, x3), (p0, p1, p2, p3)
    count, columns = x0.shape
    raw = jnp.zeros((count, 32), F32)
    for k in range(NSTREAM):
        raw = raw + lax.dot_general(xs[k][...], ps[k][...], CONTRACT_LAST, preferred_element_type=F32)
    stat[:, 0:32] = raw

    def rows(block, carry):
        here = pl.ds(pl.multiple_of(block * ROWS, ROWS), ROWS)
        total = jnp.zeros((ROWS, LANES), F32)
        for k in range(NSTREAM):
            for start in range(0, columns, LANES):
                value = xs[k][here, start : start + LANES].astype(F32)
                total = total + value * value
        stat[here, 24:25] = jnp.sum(total, axis=1, keepdims=True)
        return carry

    lax.fori_loop(0, count // ROWS, rows, 0)
    out_ref[...] = stat[...].T[0:32, :]


def mix_in_kernel(pre, x0, x1, x2, x3, gain, token_map, send, h_ref, out_ref, cols, stat, u_ref):
    xs = (x0, x1, x2, x3)
    count, columns = x0.shape
    cols[:, 0:8] = pre[...].T

    def rows(block, carry):
        here = pl.ds(pl.multiple_of(block * ROWS, ROWS), ROWS)
        weight = [jnp.broadcast_to(cols[here, k : k + 1], (ROWS, LANES)) for k in range(NSTREAM)]
        sums = [jnp.zeros((ROWS, LANES), F32) for _ in range(NSTREAM + 1)]
        for start in range(0, columns, LANES):
            span = slice(start, start + LANES)
            value = [x[here, span].astype(F32) for x in xs]
            h = weight[0] * value[0]
            for k in range(1, NSTREAM):
                h = h + weight[k] * value[k]
            for k in range(NSTREAM):
                sums[k] = sums[k] + h * value[k]
            sums[NSTREAM] = sums[NSTREAM] + h * h
            u_ref[here, span] = (h * gain[:, span].astype(F32)).astype(BF16)
            h_ref[here, span] = h.astype(BF16)
        for k in range(NSTREAM + 1):
            stat[here, k : k + 1] = jnp.sum(sums[k], axis=1, keepdims=True)
        return carry

    lax.fori_loop(0, count // ROWS, rows, 0)
    out_ref[...] = stat[...].T[0:8, :]
    for start in range(0, columns, 256):
        span = slice(start, start + 256)
        send[:, span] = jnp.dot(
            token_map[...], u_ref[:, span], preferred_element_type=F32
        ).astype(BF16)


def cot_kernel(coef, combine, moe, q_parts, x0, x1, x2, x3, y0, y1, y2, y3, pick0, pick1,
               send, e0, e1, e2, e3, out_ref, cols, stat, c0_ref, c1_ref):
    xs, ys, es = (x0, x1, x2, x3), (y0, y1, y2, y3), (e0, e1, e2, e3)
    count, columns = x0.shape
    cols[:, 0:24] = coef[...].T

    def rows(block, carry):
        here = pl.ds(pl.multiple_of(block * ROWS, ROWS), ROWS)

        def column(k):
            return jnp.broadcast_to(cols[here, k : k + 1], (ROWS, LANES))

        post = [column(k) for k in range(NSTREAM)]
        first = jnp.broadcast_to(combine[here, 0:1], (ROWS, LANES))
        second = jnp.broadcast_to(combine[here, 1:2], (ROWS, LANES))
        sums = [jnp.zeros((ROWS, LANES), F32) for _ in range(20)]
        for start in range(0, columns, LANES):
            span = slice(start, start + LANES)
            dy = [y[here, span].astype(F32) for y in ys]
            value = [x[here, span].astype(F32) for x in xs]
            out = moe[here, span].astype(F32)
            d_moe = post[0] * dy[0]
            for k in range(1, NSTREAM):
                d_moe = d_moe + post[k] * dy[k]
            c0_ref[here, span] = (first * d_moe).astype(BF16)
            c1_ref[here, span] = (second * d_moe).astype(BF16)
            for i in range(NSTREAM):
                sums[i] = sums[i] + dy[i] * out
                for j in range(NSTREAM):
                    sums[4 + 4 * i + j] = sums[4 + 4 * i + j] + dy[i] * value[j]
        for k in range(20):
            stat[here, k : k + 1] = jnp.sum(sums[k], axis=1, keepdims=True)
        mix = [column(4 + k) for k in range(16)]
        for start in range(0, columns, LANES):
            span = slice(start, start + LANES)
            dy = [y[here, span].astype(F32) for y in ys]
            for i in range(NSTREAM):
                total = mix[i] * dy[0]
                for j in range(1, NSTREAM):
                    total = total + mix[4 * j + i] * dy[j]
                es[i][here, span] = total.astype(BF16)
        return carry

    lax.fori_loop(0, count // ROWS, rows, 0)
    out_ref[...] = stat[...].T[0:24, :]
    for start in range(0, columns, 256):
        span = slice(start, start + 256)
        total = jnp.dot(pick0[...], c0_ref[:, span], preferred_element_type=F32)
        total = total + jnp.dot(pick1[...], c1_ref[:, span], preferred_element_type=F32)
        send[:, span] = total.astype(BF16)
    token_map = pick0[...] + pick1[...]
    send[:, columns : columns + LANES] = jnp.dot(
        token_map, q_parts[...], preferred_element_type=F32
    ).astype(BF16)


def hidden_kernel(order, tail, g0, g1, g2, g3, z0, z1, z2, z3, out_ref):
    width = z0.shape[1]
    for k, (both, hidden) in enumerate(((g0, z0), (g1, z1), (g2, z2), (g3, z3))):
        start = order[k] * z0.shape[0]

        def rows(block, carry):
            here = pl.ds(pl.multiple_of(block * ROWS, ROWS), ROWS)
            there = pl.ds(pl.multiple_of(start + block * ROWS, ROWS), ROWS)
            parts = tail[there, :].astype(F32)
            q = parts[:, 0:1] + parts[:, 1:2] + parts[:, 2:3]
            q = jnp.broadcast_to(q, (ROWS, 256))
            for col in range(0, width, 256):
                gate = both[here, col : col + 256].astype(F32) * q
                up = both[here, width + col : width + col + 256].astype(F32) * q
                dz = hidden[here, col : col + 256].astype(F32)
                sig = jax.nn.sigmoid(gate)
                d_gate = dz * up * sig * (1.0 + gate * (1.0 - sig))
                d_up = dz * gate * sig
                out_ref[there, col : col + 256] = d_gate.astype(BF16)
                out_ref[there, width + col : width + col + 256] = d_up.astype(BF16)
            return carry

        lax.fori_loop(0, both.shape[0] // ROWS, rows, 0)


def collect_kernel(back, token_map_t, gain, x0, x1, x2, x3, du_ref, out_ref, gu_ref, stat):
    xs = (x0, x1, x2, x3)
    count, columns = x0.shape
    for start in range(0, columns, 256):
        span = slice(start, start + 256)
        du = jnp.dot(token_map_t[...], back[:, span], preferred_element_type=F32)
        gu = du * gain[:, span].astype(F32)
        gu_ref[:, span] = gu
        du_ref[:, span] = gu.astype(BF16)

    def rows(block, carry):
        here = pl.ds(pl.multiple_of(block * ROWS, ROWS), ROWS)
        sums = [jnp.zeros((ROWS, LANES), F32) for _ in range(NSTREAM)]
        for start in range(0, columns, LANES):
            span = slice(start, start + LANES)
            gu = gu_ref[here, span]
            for k in range(NSTREAM):
                sums[k] = sums[k] + gu * xs[k][here, span].astype(F32)
        for k in range(NSTREAM):
            stat[here, k : k + 1] = jnp.sum(sums[k], axis=1, keepdims=True)
        return carry

    lax.fori_loop(0, count // ROWS, rows, 0)
    out_ref[...] = stat[...].T[0:8, :]


def final_kernel(order, a0, a1, a2, a3, small, early, u0, u1, u2, u3, h0, h1, h2, h3,
                 e0, e1, e2, e3, x0, x1, x2, x3, p0, p1, p2, p3, out_ref, cols, coef_ref):
    gus, hs, es = (u0, u1, u2, u3), (h0, h1, h2, h3), (e0, e1, e2, e3)
    xs, ps = (x0, x1, x2, x3), (p0, p1, p2, p3)
    count, columns = u0.shape
    pieces = [a[...] for a in (a0, a1, a2, a3)]
    a_part = [sum(pieces[k][(n - k) % 4 : (n - k) % 4 + 1, :] for k in range(4)) for n in range(4)]
    pre = [small[n : n + 1, :] for n in range(4)]
    b_part = [small[4 + n : 5 + n, :] for n in range(4)]
    raw = [small[8 + n : 9 + n, :] for n in range(4)]
    q, r, d_rscale, scale = (small[12 + n : 13 + n, :] for n in range(4))
    norm_dot = sum(pre[n] * a_part[n] for n in range(4))
    cube = q * q * q * (1.0 / D) * norm_dot
    coef_ref[...] = jnp.zeros(coef_ref.shape, F32)
    coef_ref[0:24, :] = early[...]
    for n in range(4):
        d_pre = q * a_part[n] - cube * b_part[n]
        d_proj = d_pre * scale * pre[n] * (1.0 - pre[n])
        d_rscale = d_rscale + d_proj * raw[n]
        coef_ref[n : n + 1, :] = r * d_proj
    coef_ref[32:33, :] = pre[0] * q
    coef_ref[33:34, :] = -pre[0] * cube
    coef_ref[34:35, :] = -(r * r * r) * (1.0 / (NSTREAM * D)) * d_rscale
    cols[...] = coef_ref[...].T
    weights = cols[:, 0:32]
    for k in range(4):
        base = pl.multiple_of(order[k] * columns, LANES)
        for start in range(0, columns, 256):
            span = slice(start, start + 256)
            total = jnp.dot(
                weights, ps[k][:, span].astype(F32), precision=lax.Precision.HIGHEST,
                preferred_element_type=F32,
            )
            total = total + es[k][:, span].astype(F32)
            total = total + cols[:, 32:33] * gus[k][:, span].astype(F32)
            total = total + cols[:, 33:34] * hs[k][:, span].astype(F32)
            total = total + cols[:, 34:35] * xs[(4 - k) % 4][:, span].astype(F32)
            out_ref[:, pl.ds(pl.multiple_of(base + start, LANES), 256)] = total.astype(BF16)


def slot_maps(expert_ids, experts, capacity):
    hits = (expert_ids[:, :, None] == jnp.arange(experts, dtype=jnp.int32)).astype(jnp.int32)
    per_token = jnp.sum(hits, axis=1)
    count = expert_ids.shape[0]
    before = (jnp.arange(count)[:, None] > jnp.arange(count)[None, :]).astype(BF16)
    earlier = jnp.dot(before, per_token.astype(BF16), preferred_element_type=F32).astype(jnp.int32)
    position = jnp.sum(hits * earlier[:, None, :], axis=2)
    slot_id = expert_ids * capacity + position
    slots = jnp.arange(experts * capacity, dtype=jnp.int32)
    pick = [(slot_id[None, :, k] == slots[:, None]).astype(BF16) for k in range(TOP)]
    back = jnp.any(slot_id[:, :, None] == slots[None, None, :], axis=1).astype(BF16)
    return pick, back


def reduce_rows(part, me):
    quarter = part.shape[0] // NSTREAM
    pieces = [
        lax.dynamic_slice_in_dim(part, (me + k) % NSTREAM * quarter, quarter, 0)
        for k in range(NSTREAM)
    ]
    total = pieces[0].astype(F32)
    for k in range(1, NSTREAM):
        total = total + shift(pieces[k], k).astype(F32)
    return total.astype(BF16)


def shards(streams, cotangent, moe_out, coef_proj, coef_scale, coef_bias, norm_gain, expert_ids,
           combine, w_gate, w_up, w_down):
    me = lax.axis_index("stream")
    count, columns = moe_out.shape
    experts = lax.axis_size("expert") // 2
    capacity = max(2, 2 * count * TOP // experts)
    order = ((me - jnp.arange(NSTREAM, dtype=jnp.int32)) % NSTREAM).astype(jnp.int32)

    table = jnp.pad(coef_proj, ((0, 0), (0, 32 - coef_proj.shape[1]), (0, 0)))

    def table_for(k):
        return lax.dynamic_index_in_dim(table, (me + k) % NSTREAM, 0, False)

    tables = [table_for(0)] + [shift(table_for(k), k) for k in range(1, NSTREAM)]

    def quarters(array):
        flat = array.reshape(count, NSTREAM * columns)
        return [
            lax.dynamic_slice_in_dim(flat, (me + k) % NSTREAM * columns, columns, 1)
            for k in range(NSTREAM)
        ]

    x_own = quarters(streams)
    x_rel = [x_own[0]] + [shift(x_own[k], k) for k in range(1, NSTREAM)]

    scratch = pltpu.VMEM((count, LANES), F32)
    backwards = [tables[(4 - k) % 4] for k in range(NSTREAM)]
    sums = call(
        project_kernel, "project", sds((32, count), F32), x_own + backwards, [scratch],
        2 * count * 32 * NSTREAM * columns,
    )
    sums = small_sum(sums)
    projected, squares = sums[0:24], sums[24]
    rscale = lax.rsqrt(squares / (NSTREAM * D) + EPSILON)
    projection = projected * rscale[None, :]
    pre = jax.nn.sigmoid(coef_scale[0] * projection[0:4] + coef_bias[0:4, None])
    pre_rel = relative(pre, me)
    pick, back_map = slot_maps(expert_ids, experts, capacity)
    slots = experts * capacity
    send_u, h_own, in_sums = call(
        mix_in_kernel, "mix_in",
        [sds((slots, columns), BF16), sds((count, columns), BF16), sds((8, count), F32)],
        [jnp.concatenate([pre_rel, pre_rel])] + x_rel + [norm_gain[None, :], pick[0] + pick[1]],
        [scratch, scratch, pltpu.VMEM((count, columns), BF16)],
        2 * slots * count * columns,
    )

    def to_experts(array):
        blocks = array.reshape(2 * experts, slots // (2 * experts), array.shape[1])
        moved = lax.all_to_all(blocks, "expert", split_axis=0, concat_axis=0, tiled=True)
        return moved.reshape(array.shape)

    rows_u = to_experts(send_u)

    swap = [(i, i ^ 1) for i in range(2 * experts)]

    def sibling(array):
        return lax.ppermute(array, "expert", swap)

    w_both = jnp.concatenate([w_gate, sibling(w_gate), w_up, sibling(w_up)], axis=1)
    wide = columns + LANES
    w_hidden = jnp.concatenate([w_down, sibling(w_down)], axis=0)
    w_hidden = jnp.pad(w_hidden, ((0, 0), (0, LANES)))

    cotangent, _ = lax.optimization_barrier((cotangent, x_rel[1]))
    y_own = quarters(cotangent)
    y_rel = [y_own[0]] + [shift(y_own[k], k) for k in range(1, NSTREAM)]

    in_sums = jnp.concatenate([relative(in_sums[0:4], me), in_sums[4:8]])
    in_sums = small_sum(in_sums)
    b_part, square_sum = in_sums[0:4], in_sums[4]
    qscale = lax.rsqrt(square_sum / D + EPSILON)
    q_high = qscale.astype(BF16)
    q_rest = qscale - q_high.astype(F32)
    q_mid = q_rest.astype(BF16)
    q_low = (q_rest - q_mid.astype(F32)).astype(BF16)
    q_parts = jnp.pad(jnp.stack([q_high, q_mid, q_low], axis=1), ((0, 0), (0, LANES - 3)))

    def later(values):
        post = 2.0 * jax.nn.sigmoid(coef_scale[1] * values[4:8] + coef_bias[4:8, None])
        return post, sinkhorn(coef_scale[2] * values[8:] + coef_bias[8:, None])

    (post, mixing), pullback = jax.vjp(later, projection)
    mix_rel = relative(relative(mixing, me, 0), me, 1).reshape(16, count)
    coef = jnp.concatenate([relative(post, me), mix_rel, jnp.zeros((4, count), F32)])
    half = pltpu.VMEM((count, columns), BF16)
    piece = sds((count, columns), BF16)
    send_c, *grad_mix, cot_sums = call(
        cot_kernel, "cot",
        [sds((slots, wide), BF16), piece, piece, piece, piece, sds((24, count), F32)],
        [coef, combine, moe_out, q_parts] + x_rel + y_rel + pick,
        [scratch, scratch, half, half],
        4 * slots * count * columns,
    )
    rows_c = to_experts(send_c)

    part_both = jnp.dot(rows_u, w_both, preferred_element_type=F32).astype(BF16)
    both = spread(reduce_rows(part_both, me))
    part_hidden = lax.dot_general(rows_c, w_hidden, CONTRACT_LAST, preferred_element_type=F32)
    hidden = spread(reduce_rows(part_hidden.astype(BF16), me))
    d_both = hidden_call(order, rows_c[:, columns:], both, hidden, part_both.shape)
    part_du = lax.dot_general(d_both, w_both, CONTRACT_LAST, preferred_element_type=F32)
    back = to_experts(part_du.astype(BF16))

    h_own, cot_sums, *grad_mix, _ = lax.optimization_barrier((h_own, cot_sums, *grad_mix, d_both))
    h_rel = spread(h_own)
    e_rel = [grad_mix[0]] + [shift(grad_mix[(4 - k) % 4], k) for k in range(1, NSTREAM)]
    post_dots = relative(cot_sums[0:4], me)
    mix_dots = cot_sums[4:20].reshape(NSTREAM, NSTREAM, count)
    mix_dots = relative(relative(mix_dots, me, 0), me, 1).reshape(16, count)
    cot_sums = small_sum(jnp.concatenate([post_dots, mix_dots, jnp.zeros((4, count), F32)]))
    (d_proj,) = pullback((cot_sums[0:4], cot_sums[4:20].reshape(NSTREAM, NSTREAM, count)))
    early_rscale = jnp.sum(d_proj * projected, axis=0)
    early = rscale[None, :] * d_proj
    small = jnp.concatenate(
        [pre_rel, relative(b_part, me), relative(projected[0:4], me), qscale[None],
         rscale[None], early_rscale[None], jnp.broadcast_to(coef_scale[0:1, None], (1, count))]
    )
    final_tables = [
        jnp.concatenate([relative(t[0:4], me), t[4:24], jnp.zeros((8, columns), BF16)])
        for t in tables
    ]
    gu_own, last_sums = call(
        collect_kernel, "collect", [piece, sds((8, count), F32)],
        [back, back_map, norm_gain[None, :]] + x_rel,
        [pltpu.VMEM((count, columns), F32), scratch],
        2 * slots * count * columns,
    )
    gu_rel = spread(gu_own)
    last = spread(last_sums)
    grads = final_call(order, last, small, early, gu_rel, h_rel, e_rel, x_own, final_tables)
    return grads.reshape(streams.shape)


def hidden_call(order, tail, both, hidden, shape):
    args = [tail] + both + hidden
    return pl.pallas_call(
        hidden_kernel,
        out_shape=sds(shape, BF16),
        in_specs=[pl.BlockSpec(memory_space=pltpu.SMEM)] + whole(len(args)),
        out_specs=whole(1)[0],
        compiler_params=pltpu.CompilerParams(vmem_limit_bytes=VMEM_LIMIT),
        name="hidden",
    )(order, *args)


def final_call(order, last, small, early, gu_rel, h_rel, e_rel, x_own, tables):
    args = last + [small, early] + gu_rel + h_rel + e_rel + x_own + tables
    count, columns = x_own[0].shape
    return pl.pallas_call(
        final_kernel,
        out_shape=sds((count, NSTREAM * columns), BF16),
        in_specs=[pl.BlockSpec(memory_space=pltpu.SMEM)] + whole(len(args)),
        out_specs=whole(1)[0],
        scratch_shapes=[pltpu.VMEM((count, LANES), F32), pltpu.VMEM((LANES, count), F32)],
        compiler_params=pltpu.CompilerParams(vmem_limit_bytes=VMEM_LIMIT),
        name="final",
    )(order, *args)


def solution(mesh):
    placed = (
        P("expert", "stream", None),
        P("expert", "stream", None),
        P("expert", "stream"),
        P(None, None, "stream"),
        P(),
        P(),
        P("stream"),
        P("expert", None),
        P("expert", None),
        P("stream", "expert"),
        P("stream", "expert"),
        P("expert", "stream"),
    )
    return jax.shard_map(
        shards, mesh=mesh, in_specs=placed, out_specs=P("expert", "stream", None), check_vma=False
    )
```

```python
import jax
import jax.numpy as jnp
from jax import lax
from jax.experimental import pallas as pl
from jax.experimental.pallas import tpu as pltpu
from jax.sharding import PartitionSpec as P

D = 7168
NSTREAM = 4
SINK = 4
TOP = 2
EPSILON = 1e-06
F32 = jnp.float32
BF16 = jnp.bfloat16
ROWS = 16
LANES = 128
VMEM_LIMIT = 60 * 1024 * 1024
CONTRACT_LAST = (((1,), (1,)), ((), ()))


def sinkhorn(logits):
    mixing = jnp.exp(logits).reshape(NSTREAM, NSTREAM, -1)
    for iteration in range(SINK):
        mixing = mixing / jnp.sum(mixing, axis=1, keepdims=True)
        mixing = mixing / jnp.sum(mixing, axis=0, keepdims=True)
    return mixing


def relative(array, me, axis=0):
    flipped = jnp.flip(array, axis)
    doubled = jnp.concatenate([flipped, flipped], axis)
    return lax.dynamic_slice_in_dim(doubled, NSTREAM - 1 - me, NSTREAM, axis)


def shift(array, step):
    pairs = [(i, (i + step) % NSTREAM) for i in range(NSTREAM)]
    return lax.ppermute(array, "stream", pairs)


def small_sum(array):
    return array + shift(array, 1) + shift(array, 2) + shift(array, 3)


def spread(array):
    return [array, shift(array, 1), shift(array, 2), shift(array, 3)]


def whole(count):
    return [pl.BlockSpec(memory_space=pltpu.VMEM)] * count


def call(kernel, name, out_shape, args, scratch=(), flops=0, smem=0, anywhere=False, hbm_outs=0):
    single = not isinstance(out_shape, (list, tuple))
    outs = [out_shape] if single else list(out_shape)
    moved = sum(a.size * a.dtype.itemsize for a in list(args) + outs)
    place = [pl.BlockSpec(memory_space=pl.ANY)] if anywhere else whole(1)
    specs = [pl.BlockSpec(memory_space=pltpu.SMEM)] * smem + place * (len(args) - smem)
    out_place = [pl.BlockSpec(memory_space=pl.ANY)] * hbm_outs + place * (len(outs) - hbm_outs)
    return pl.pallas_call(
        kernel,
        out_shape=out_shape,
        in_specs=specs,
        out_specs=out_place[0] if single else out_place,
        scratch_shapes=list(scratch),
        compiler_params=pltpu.CompilerParams(vmem_limit_bytes=VMEM_LIMIT),
        cost_estimate=pl.CostEstimate(flops=flops, bytes_accessed=moved, transcendentals=0),
        name=name,
    )(*args)


def sds(shape, dtype):
    return jax.ShapeDtypeStruct(shape, dtype)


def project_kernel(order, x_ref, p0, p1, p2, p3, out_ref, stat):
    count, columns = x_ref.shape[0], p0.shape[1]
    raw = jnp.zeros((count, 32), F32)
    for k, table in enumerate((p0, p1, p2, p3)):
        here = pl.ds(pl.multiple_of(order[k] * columns, LANES), columns)
        raw = raw + lax.dot_general(
            x_ref[:, here], table[...], CONTRACT_LAST, preferred_element_type=F32
        )
    stat[:, 0:32] = raw

    def rows(block, carry):
        here = pl.ds(pl.multiple_of(block * ROWS, ROWS), ROWS)
        total = jnp.zeros((ROWS, LANES), F32)
        for start in range(0, x_ref.shape[1], LANES):
            value = x_ref[here, start : start + LANES].astype(F32)
            total = total + value * value
        stat[here, 24:25] = jnp.sum(total, axis=1, keepdims=True)
        return carry

    lax.fori_loop(0, count // ROWS, rows, 0)
    out_ref[...] = stat[...].T[0:32, :]


def mix_in_kernel(scale, bias, s0, s1, s2, s3, x_ref, gain, token_map, send, h_ref, out_ref,
                  cols, stat, u_ref, o_buf, o_sem):
    xs = [x_ref.at[k] for k in range(NSTREAM)]
    count, columns = xs[0].shape
    total = s0[...] + s1[...] + s2[...] + s3[...]
    rscale = lax.rsqrt(total[24:25, :] * (1.0 / (NSTREAM * D)) + EPSILON)
    logits = [scale[0] * (total[k : k + 1, :] * rscale) + bias[k] for k in range(NSTREAM)]
    pre = jax.nn.sigmoid(jnp.concatenate(logits + logits, axis=0))
    cols[:, 0:8] = pre.T

    def rows(block, carry):
        here = pl.ds(pl.multiple_of(block * ROWS, ROWS), ROWS)
        weight = [jnp.broadcast_to(cols[here, k : k + 1], (ROWS, LANES)) for k in range(NSTREAM)]
        sums = [jnp.zeros((ROWS, LANES), F32) for _ in range(NSTREAM + 1)]
        for start in range(0, columns, LANES):
            span = slice(start, start + LANES)
            value = [x[here, span].astype(F32) for x in xs]
            h = weight[0] * value[0]
            for k in range(1, NSTREAM):
                h = h + weight[k] * value[k]
            for k in range(NSTREAM):
                sums[k] = sums[k] + h * value[k]
            sums[NSTREAM] = sums[NSTREAM] + h * h
            u_ref[here, span] = (h * gain[:, span].astype(F32)).astype(BF16)
            h_ref[here, span] = h.astype(BF16)
        for k in range(NSTREAM + 1):
            stat[here, k : k + 1] = jnp.sum(sums[k], axis=1, keepdims=True)
        return carry

    lax.fori_loop(0, count // ROWS, rows, 0)
    out_ref[...] = stat[...].T[0:8, :]
    send_chunks(send, o_buf, o_sem, columns, lambda span: jnp.dot(
        token_map[...], u_ref[:, span], preferred_element_type=F32
    ))


def send_chunks(out_ref, o_buf, o_sem, columns, product):
    copies = []
    for c in range(columns // 256):
        span = slice(c * 256, c * 256 + 256)
        o_buf[:, span] = product(span).astype(BF16)
        copies.append(pltpu.make_async_copy(o_buf.at[:, span], out_ref.at[:, span], o_sem.at[c]))
        copies[c].start()
    for copy in copies:
        copy.wait()


def cot_kernel(coef, combine, moe, q_parts, x_ref, y0, y1, y2, y3, pick0, pick1,
               send, e0, e1, e2, e3, out_ref, cols, stat, c0_ref, c1_ref):
    xs, ys, es = [x_ref.at[k] for k in range(NSTREAM)], (y0, y1, y2, y3), (e0, e1, e2, e3)
    count, columns = y0.shape
    cols[:, 0:24] = coef[...].T

    def rows(block, carry):
        here = pl.ds(pl.multiple_of(block * ROWS, ROWS), ROWS)

        def column(k):
            return jnp.broadcast_to(cols[here, k : k + 1], (ROWS, LANES))

        post = [column(k) for k in range(NSTREAM)]
        first = jnp.broadcast_to(combine[here, 0:1], (ROWS, LANES))
        second = jnp.broadcast_to(combine[here, 1:2], (ROWS, LANES))
        sums = [jnp.zeros((ROWS, LANES), F32) for _ in range(20)]
        for start in range(0, columns, LANES):
            span = slice(start, start + LANES)
            dy = [y[here, span].astype(F32) for y in ys]
            value = [x[here, span].astype(F32) for x in xs]
            out = moe[here, span].astype(F32)
            d_moe = post[0] * dy[0]
            for k in range(1, NSTREAM):
                d_moe = d_moe + post[k] * dy[k]
            c0_ref[here, span] = (first * d_moe).astype(BF16)
            c1_ref[here, span] = (second * d_moe).astype(BF16)
            for i in range(NSTREAM):
                sums[i] = sums[i] + dy[i] * out
                for j in range(NSTREAM):
                    sums[4 + 4 * i + j] = sums[4 + 4 * i + j] + dy[i] * value[j]
        for k in range(20):
            stat[here, k : k + 1] = jnp.sum(sums[k], axis=1, keepdims=True)
        mix = [column(4 + k) for k in range(16)]
        for start in range(0, columns, LANES):
            span = slice(start, start + LANES)
            dy = [y[here, span].astype(F32) for y in ys]
            for i in range(NSTREAM):
                total = mix[i] * dy[0]
                for j in range(1, NSTREAM):
                    total = total + mix[4 * j + i] * dy[j]
                es[i][here, span] = total.astype(BF16)
        return carry

    lax.fori_loop(0, count // ROWS, rows, 0)
    out_ref[...] = stat[...].T[0:24, :]
    for start in range(0, columns, 256):
        span = slice(start, start + 256)
        total = jnp.dot(pick0[...], c0_ref[:, span], preferred_element_type=F32)
        total = total + jnp.dot(pick1[...], c1_ref[:, span], preferred_element_type=F32)
        send[:, span] = total.astype(BF16)
    token_map = pick0[...] + pick1[...]
    send[:, columns : columns + LANES] = jnp.dot(
        token_map, q_parts[...], preferred_element_type=F32
    ).astype(BF16)


def product_kernel(order, *refs):
    *pieces, w_ref, out_ref, rows_ref = refs
    rows = pieces[0].shape[0]

    @pl.when(pl.program_id(0) == 0)
    def join():
        for k, piece in enumerate(pieces):
            here = pl.ds(pl.multiple_of(order[k] * rows, rows), rows)
            rows_ref[here, :] = piece[...]

    total = lax.dot_general(rows_ref[...], w_ref[...], CONTRACT_LAST, preferred_element_type=F32)
    out_ref[...] = total.astype(BF16)


def product(order, pieces, weights, name):
    rows, depth = pieces[0].shape
    columns = weights.shape[0]
    whole_piece = pl.BlockSpec((rows, depth), lambda j: (0, 0))
    return pl.pallas_call(
        product_kernel,
        out_shape=sds((rows * len(pieces), columns), BF16),
        grid=(columns // 256,),
        in_specs=[pl.BlockSpec(memory_space=pltpu.SMEM)] + [whole_piece] * len(pieces)
        + [pl.BlockSpec((256, depth), lambda j: (j, 0))],
        out_specs=pl.BlockSpec((rows * len(pieces), 256), lambda j: (0, j)),
        scratch_shapes=[pltpu.VMEM((rows * len(pieces), depth), BF16)],
        compiler_params=pltpu.CompilerParams(vmem_limit_bytes=VMEM_LIMIT),
        cost_estimate=pl.CostEstimate(
            flops=2 * rows * len(pieces) * depth * columns,
            bytes_accessed=2 * columns * depth + 4 * rows * len(pieces) * columns,
            transcendentals=0,
        ),
        name=name,
    )(order, *pieces, weights)


def hidden_kernel(tail, both, z_ref, out_ref):
    count, width = both.shape[0], z_ref.shape[2]

    def rows(block, carry):
        here = pl.ds(pl.multiple_of(block * ROWS, ROWS), ROWS)
        parts = tail[here, :].astype(F32)
        q = jnp.broadcast_to(parts[:, 0:1] + parts[:, 1:2] + parts[:, 2:3], (ROWS, 256))
        for col in range(0, width, 256):
            gate = both[here, col : col + 256].astype(F32) * q
            up = both[here, width + col : width + col + 256].astype(F32) * q
            dz = z_ref[0, here, col : col + 256].astype(F32)
            for k in range(1, NSTREAM):
                dz = dz + z_ref[k, here, col : col + 256].astype(F32)
            sig = jax.nn.sigmoid(gate)
            d_gate = dz * up * sig * (1.0 + gate * (1.0 - sig))
            d_up = dz * gate * sig
            out_ref[here, col : col + 256] = d_gate.astype(BF16)
            out_ref[here, width + col : width + col + 256] = d_up.astype(BF16)
        return carry

    lax.fori_loop(0, count // ROWS, rows, 0)


def collect_kernel(back, token_map_t, gain, x_ref, out_ref, gu_ref, stat):
    count, columns = gu_ref.shape
    for start in range(0, columns, 256):
        span = slice(start, start + 256)
        du = jnp.dot(token_map_t[...], back[:, span], preferred_element_type=F32)
        gu = du * gain[:, span].astype(F32)
        gu_ref[:, span] = gu
        out_ref[:, span] = gu.astype(BF16)
    stat[...] = jnp.zeros(stat.shape, F32)

    def rows(block, carry):
        here = pl.ds(pl.multiple_of(block * ROWS, ROWS), ROWS)
        sums = [jnp.zeros((ROWS, LANES), F32) for _ in range(NSTREAM)]
        for start in range(0, columns, LANES):
            span = slice(start, start + LANES)
            gu = gu_ref[here, span]
            for k in range(NSTREAM):
                sums[k] = sums[k] + gu * x_ref[k, here, span].astype(F32)
        for k in range(NSTREAM):
            rest = jnp.sum(sums[k], axis=1, keepdims=True)
            for part in range(3):
                term = rest.astype(BF16).astype(F32)
                stat[here, 3 * k + part : 3 * k + part + 1] = term
                rest = rest - term
        return carry

    lax.fori_loop(0, count // ROWS, rows, 0)
    out_ref[:, columns : columns + LANES] = stat[...].astype(BF16)


def three_parts(rest):
    parts = []
    for part in range(3):
        parts.append(rest.astype(BF16).astype(F32))
        rest = rest - parts[part]
    return parts


def final_kernel(order, small, early, x_ref, u0, u1, u2, u3, h0, h1, h2, h3,
                 e0, e1, e2, e3, p0, p1, p2, p3, out_ref,
                 cols, coef_ref, s_buf, d_buf, u_buf, h_buf, e_buf, x_buf, p_buf, o_buf,
                 s_sem, in_sem, o_sem):
    count, columns = e0.shape
    us, hs, es, ps = (u0, u1, u2, u3), (h0, h1, h2, h3), (e0, e1, e2, e3), (p0, p1, p2, p3)
    firsts = [
        pltpu.make_async_copy(small, s_buf, s_sem.at[0]),
        pltpu.make_async_copy(early, d_buf, s_sem.at[1]),
    ]
    where = [pl.ds(pl.multiple_of(order[k] * columns, LANES), columns) for k in range(4)]
    grads = [pltpu.make_async_copy(us[k], u_buf.at[k], in_sem.at[k, 0]) for k in range(4)]
    others = [
        [
            pltpu.make_async_copy(es[k], e_buf.at[k], in_sem.at[k, 1]),
            pltpu.make_async_copy(hs[k], h_buf.at[k], in_sem.at[k, 3]),
            pltpu.make_async_copy(x_ref.at[:, where[k]], x_buf.at[k], in_sem.at[k, 4]),
        ] + [
            pltpu.make_async_copy(
                ps[k], p_buf.at[k, pl.ds(32 * part, 32), :], in_sem.at[k, 5 + part]
            )
            for part in range(3)
        ]
        for k in range(4)
    ]
    for copy in firsts + grads + others[0] + others[1] + others[2] + others[3]:
        copy.start()
    for copy in firsts:
        copy.wait()
    coef_ref[...] = jnp.zeros(coef_ref.shape, F32)
    for part, term in enumerate(three_parts(d_buf[...])):
        coef_ref[32 * part : 32 * part + 24, :] = term
    coef_ref[96:120, :] = s_buf[...]
    cols[...] = coef_ref[...].T
    for copy in grads:
        copy.wait()
    sums = u_buf[0, :, columns : columns + LANES].astype(F32)
    for k in range(1, NSTREAM):
        sums = sums + u_buf[k, :, columns : columns + LANES].astype(F32)
    a_part = [
        sums[:, 3 * n : 3 * n + 1] + sums[:, 3 * n + 1 : 3 * n + 2] + sums[:, 3 * n + 2 : 3 * n + 3]
        for n in range(NSTREAM)
    ]
    pre = [cols[:, 96 + n : 97 + n] for n in range(4)]
    b_part = [cols[:, 100 + n : 101 + n] for n in range(4)]
    raw = [cols[:, 104 + n : 105 + n] for n in range(4)]
    q, r, d_rscale, scale = (cols[:, 108 + n : 109 + n] for n in range(4))
    norm_dot = pre[0] * a_part[0]
    for n in range(1, 4):
        norm_dot = norm_dot + pre[n] * a_part[n]
    cube = q * q * q * (1.0 / D) * norm_dot
    for n in range(4):
        d_pre = q * a_part[n] - cube * b_part[n]
        d_proj = d_pre * scale * pre[n] * (1.0 - pre[n])
        d_rscale = d_rscale + d_proj * raw[n]
        for part, term in enumerate(three_parts(r * d_proj)):
            cols[:, 32 * part + n : 32 * part + n + 1] = term
    own = cols[:, 112:113]
    by_u = jnp.broadcast_to(own * q, (count, 256))
    by_h = jnp.broadcast_to(-own * cube, (count, 256))
    by_x = jnp.broadcast_to(-(r * r * r) * (1.0 / (NSTREAM * D)) * d_rscale, (count, 256))
    weights = cols[:, 0:96].astype(BF16)
    outs = []
    for k in range(4):
        for copy in others[k]:
            copy.wait()
        for start in range(0, columns, 256):
            span = slice(start, start + 256)
            total = jnp.dot(weights, p_buf[k, :, span], preferred_element_type=F32)
            total = total + e_buf[k, :, span].astype(F32)
            total = total + by_u * u_buf[k, :, span].astype(F32)
            total = total + by_h * h_buf[k, :, span].astype(F32)
            total = total + by_x * x_buf[k, :, span].astype(F32)
            o_buf[k, :, span] = total.astype(BF16)
        outs.append(pltpu.make_async_copy(o_buf.at[k], out_ref.at[:, where[k]], o_sem.at[k]))
        outs[k].start()
    for copy in outs:
        copy.wait()


def slot_maps(expert_ids, experts, capacity):
    hits = (expert_ids[:, :, None] == jnp.arange(experts, dtype=jnp.int32)).astype(jnp.int32)
    per_token = jnp.sum(hits, axis=1)
    count = expert_ids.shape[0]
    before = (jnp.arange(count)[:, None] > jnp.arange(count)[None, :]).astype(BF16)
    earlier = jnp.dot(before, per_token.astype(BF16), preferred_element_type=F32).astype(jnp.int32)
    position = jnp.sum(hits * earlier[:, None, :], axis=2)
    slot_id = expert_ids * capacity + position
    slots = jnp.arange(experts * capacity, dtype=jnp.int32)
    pick = [(slot_id[None, :, k] == slots[:, None]).astype(BF16) for k in range(TOP)]
    back = jnp.any(slot_id[:, :, None] == slots[None, None, :], axis=1).astype(BF16)
    return pick, back


def reduce_rows(part, me):
    quarter = part.shape[0] // NSTREAM
    pieces = [
        lax.dynamic_slice_in_dim(part, (me + k) % NSTREAM * quarter, quarter, 0)
        for k in range(NSTREAM)
    ]
    total = pieces[0].astype(F32)
    for k in range(1, NSTREAM):
        total = total + shift(pieces[k], k).astype(F32)
    return total.astype(BF16)


def shards(streams, cotangent, moe_out, coef_proj, coef_scale, coef_bias, norm_gain, expert_ids,
           combine, w_gate, w_up, w_down):
    me = lax.axis_index("stream")
    count, columns = moe_out.shape
    experts = lax.axis_size("expert") // 2
    capacity = max(2, 2 * count * TOP // experts)
    order = ((me - jnp.arange(NSTREAM, dtype=jnp.int32)) % NSTREAM).astype(jnp.int32)

    table = jnp.pad(coef_proj, ((0, 0), (0, 32 - coef_proj.shape[1]), (0, 0)))

    def table_for(k):
        return lax.dynamic_index_in_dim(table, (me + k) % NSTREAM, 0, False)

    tables = [table_for(0)] + [shift(table_for(k), k) for k in range(1, NSTREAM)]

    x_flat = streams.reshape(count, NSTREAM * columns)
    x_send = jnp.stack([x_flat[:, k * columns : (k + 1) * columns] for k in range(NSTREAM)])
    x_all = lax.all_to_all(x_send, "stream", split_axis=0, concat_axis=0, tiled=True)

    scratch = pltpu.VMEM((count, LANES), F32)
    sums = call(
        project_kernel, "project", sds((32, count), F32), [order, x_flat] + tables, [scratch],
        2 * count * 32 * NSTREAM * columns, smem=1,
    )
    sums = spread(sums)
    partial_sums = sums
    sums = sums[0] + sums[1] + sums[2] + sums[3]
    projected, squares = sums[0:24], sums[24]
    rscale = lax.rsqrt(squares / (NSTREAM * D) + EPSILON)
    projection = projected * rscale[None, :]
    pre = jax.nn.sigmoid(coef_scale[0] * projection[0:4] + coef_bias[0:4, None])
    pick, back_map = slot_maps(expert_ids, experts, capacity)
    slots = experts * capacity
    chunks = columns // 256
    dma = pltpu.SemaphoreType.DMA
    send_u, h_own, in_sums = call(
        mix_in_kernel, "mix_in",
        [sds((slots, columns), BF16), sds((count, columns), BF16), sds((8, count), F32)],
        [coef_scale, coef_bias] + partial_sums + [x_all, norm_gain[None, :], pick[0] + pick[1]],
        [
            scratch, scratch, pltpu.VMEM((count, columns), BF16),
            pltpu.VMEM((slots, columns), BF16), dma((chunks,)),
        ],
        2 * slots * count * columns, smem=2, hbm_outs=1,
    )

    def to_experts(array):
        blocks = array.reshape(2 * experts, slots // (2 * experts), array.shape[1])
        moved = lax.all_to_all(blocks, "expert", split_axis=0, concat_axis=0, tiled=True)
        return moved.reshape(array.shape)

    rows_u = to_experts(send_u)

    swap = [(i, i ^ 1) for i in range(2 * experts)]

    def sibling(array):
        return lax.ppermute(array, "expert", swap)

    w_both = jnp.concatenate([w_gate, sibling(w_gate), w_up, sibling(w_up)], axis=1)
    wide = columns + LANES
    w_hidden = jnp.concatenate([w_down, sibling(w_down)], axis=0)
    w_hidden = jnp.pad(w_hidden, ((0, 0), (0, LANES)))

    y_flat = cotangent.reshape(count, NSTREAM * columns)
    y_own = [
        lax.dynamic_slice_in_dim(y_flat, (me + k) % NSTREAM * columns, columns, 1)
        for k in range(NSTREAM)
    ]
    *y_own, in_sums = lax.optimization_barrier((*y_own, in_sums))
    y_rel = [y_own[0]] + [shift(y_own[k], k) for k in range(1, NSTREAM)]

    in_sums = small_sum(in_sums)
    b_part, square_sum = in_sums[0:4], in_sums[4]
    qscale = lax.rsqrt(square_sum / D + EPSILON)
    q_high = qscale.astype(BF16)
    q_rest = qscale - q_high.astype(F32)
    q_mid = q_rest.astype(BF16)
    q_low = (q_rest - q_mid.astype(F32)).astype(BF16)
    q_parts = jnp.pad(jnp.stack([q_high, q_mid, q_low], axis=1), ((0, 0), (0, LANES - 3)))

    def later(values):
        post = 2.0 * jax.nn.sigmoid(coef_scale[1] * values[4:8] + coef_bias[4:8, None])
        return post, sinkhorn(coef_scale[2] * values[8:] + coef_bias[8:, None])

    (post, mixing), pullback = jax.vjp(later, projection)
    mix_rel = relative(relative(mixing, me, 0), me, 1).reshape(16, count)
    coef = jnp.concatenate([relative(post, me), mix_rel, jnp.zeros((4, count), F32)])
    half = pltpu.VMEM((count, columns), BF16)
    piece = sds((count, columns), BF16)
    moe_out, w_both, w_hidden = lax.optimization_barrier((moe_out, w_both, w_hidden))
    send_c, *grad_mix, cot_sums = call(
        cot_kernel, "cot",
        [sds((slots, wide), BF16), piece, piece, piece, piece, sds((24, count), F32)],
        [coef, combine, moe_out, q_parts, x_all] + y_rel + pick,
        [scratch, scratch, half, half],
        4 * slots * count * columns,
    )
    rows_c = to_experts(send_c)
    h_own, *_ = lax.optimization_barrier((h_own, y_rel[1], y_rel[2], y_rel[3]))
    h_rel = [h_own, shift(h_own, 1), None, shift(h_own, 3)]

    part_both = jnp.dot(rows_u, w_both, preferred_element_type=F32).astype(BF16)
    both = reduce_rows(part_both, me)
    rows_c, both, h_rel[1], h_rel[3] = lax.optimization_barrier((rows_c, both, h_rel[1], h_rel[3]))
    none = jnp.zeros((1,), jnp.int32)
    part_hidden = product(none, [rows_c], w_hidden, "hidden_product")
    quarter = slots // NSTREAM
    hidden = part_hidden.reshape(NSTREAM, quarter, -1)
    hidden = lax.all_to_all(hidden, "stream", split_axis=0, concat_axis=0, tiled=True)
    tail = lax.dynamic_slice(rows_c, (me * quarter, columns), (quarter, LANES))
    d_both = call(hidden_kernel, "hidden", sds(both.shape, BF16), [tail, both, hidden])
    d_both = spread(d_both)
    part_du = product(order, d_both, w_both, "input_product")
    back = to_experts(part_du)

    *grad_mix, h_own, _, _, _, _ = lax.optimization_barrier((*grad_mix, h_own, *d_both))
    h_rel[2] = shift(h_own, 2)
    e_rel = [grad_mix[0]] + [shift(grad_mix[(4 - k) % 4], k) for k in range(1, NSTREAM)]
    post_dots = relative(cot_sums[0:4], me)
    mix_dots = relative(cot_sums[4:20].reshape(NSTREAM, NSTREAM, count), me).reshape(16, count)
    cot_sums = small_sum(jnp.concatenate([post_dots, mix_dots, jnp.zeros((4, count), F32)]))
    (d_proj,) = pullback((cot_sums[0:4], cot_sums[4:20].reshape(NSTREAM, NSTREAM, count)))
    early_rscale = jnp.sum(d_proj * projected, axis=0)
    early = rscale[None, :] * d_proj
    small = jnp.concatenate(
        [pre, b_part, projected[0:4], qscale[None], rscale[None], early_rscale[None],
         jnp.broadcast_to(coef_scale[0:1, None], (1, count)),
         lax.dynamic_slice_in_dim(pre, me, 1, 0), jnp.zeros((7, count), F32)]
    )
    back, h_rel[2], *e_rel = lax.optimization_barrier((back, h_rel[2], *e_rel))
    gu_own = call(
        collect_kernel, "collect", sds((count, wide), BF16),
        [back, back_map, norm_gain[None, :], x_all],
        [pltpu.VMEM((count, columns), F32), scratch],
        2 * slots * count * columns,
    )
    gu_rel = spread(gu_own)
    four = pltpu.VMEM((NSTREAM, count, columns), BF16)
    grads = call(
        final_kernel, "final", sds((count, NSTREAM * columns), BF16),
        [order, small, early, x_flat] + gu_rel + h_rel + e_rel + tables,
        [
            scratch, pltpu.VMEM((LANES, count), F32), pltpu.VMEM((24, count), F32),
            pltpu.VMEM((24, count), F32), pltpu.VMEM((NSTREAM, count, wide), BF16), four, four, four,
            pltpu.VMEM((NSTREAM, 96, columns), BF16), four,
            dma((2,)), dma((NSTREAM, 8)), dma((NSTREAM,)),
        ],
        2 * count * 96 * NSTREAM * columns, smem=1, anywhere=True,
    )
    return grads.reshape(streams.shape)


def solution(mesh):
    placed = (
        P("expert", "stream", None),
        P("expert", "stream", None),
        P("expert", "stream"),
        P(None, None, "stream"),
        P(),
        P(),
        P("stream"),
        P("expert", None),
        P("expert", None),
        P("stream", "expert"),
        P("stream", "expert"),
        P("expert", "stream"),
    )
    return jax.shard_map(
        shards, mesh=mesh, in_specs=placed, out_specs=P("expert", "stream", None), check_vma=False
    )
```

```python
import jax
import jax.numpy as jnp
from jax import lax
from jax.experimental import pallas as pl
from jax.experimental.pallas import tpu as pltpu
from jax.sharding import PartitionSpec as P

D = 7168
NSTREAM = 4
SINK = 4
TOP = 2
EPSILON = 1e-06
F32 = jnp.float32
BF16 = jnp.bfloat16
ROWS = 16
LANES = 128
VMEM_LIMIT = 60 * 1024 * 1024
CONTRACT_LAST = (((1,), (1,)), ((), ()))


def sinkhorn(logits):
    mixing = jnp.exp(logits).reshape(NSTREAM, NSTREAM, -1)
    for iteration in range(SINK):
        mixing = mixing / jnp.sum(mixing, axis=1, keepdims=True)
        mixing = mixing / jnp.sum(mixing, axis=0, keepdims=True)
    return mixing


def relative(array, me, axis=0):
    flipped = jnp.flip(array, axis)
    doubled = jnp.concatenate([flipped, flipped], axis)
    return lax.dynamic_slice_in_dim(doubled, NSTREAM - 1 - me, NSTREAM, axis)


def shift(array, step):
    pairs = [(i, (i + step) % NSTREAM) for i in range(NSTREAM)]
    return lax.ppermute(array, "stream", pairs)


def small_sum(array):
    return array + shift(array, 1) + shift(array, 2) + shift(array, 3)


def spread(array):
    return [array, shift(array, 1), shift(array, 2), shift(array, 3)]


def whole(count):
    return [pl.BlockSpec(memory_space=pltpu.VMEM)] * count


def call(kernel, name, out_shape, args, scratch=(), flops=0, smem=0, anywhere=False, hbm_outs=0, limit=60):
    single = not isinstance(out_shape, (list, tuple))
    outs = [out_shape] if single else list(out_shape)
    moved = sum(a.size * a.dtype.itemsize for a in list(args) + outs)
    place = [pl.BlockSpec(memory_space=pl.ANY)] if anywhere else whole(1)
    specs = [pl.BlockSpec(memory_space=pltpu.SMEM)] * smem + place * (len(args) - smem)
    out_place = [pl.BlockSpec(memory_space=pl.ANY)] * hbm_outs + place * (len(outs) - hbm_outs)
    return pl.pallas_call(
        kernel,
        out_shape=out_shape,
        in_specs=specs,
        out_specs=out_place[0] if single else out_place,
        scratch_shapes=list(scratch),
        compiler_params=pltpu.CompilerParams(vmem_limit_bytes=limit * 1024 * 1024),
        cost_estimate=pl.CostEstimate(flops=flops, bytes_accessed=moved, transcendentals=0),
        name=name,
    )(*args)


def sds(shape, dtype):
    return jax.ShapeDtypeStruct(shape, dtype)


def squares_kernel(x_ref, out_ref, stat):
    def rows(block, carry):
        here = pl.ds(pl.multiple_of(block * ROWS, ROWS), ROWS)
        total = jnp.zeros((ROWS, LANES), F32)
        for start in range(0, x_ref.shape[1], LANES):
            value = x_ref[here, start : start + LANES].astype(F32)
            total = total + value * value
        stat[here, 0:1] = jnp.sum(total, axis=1, keepdims=True)
        return carry

    lax.fori_loop(0, x_ref.shape[0] // ROWS, rows, 0)
    out_ref[...] = stat[...].T[0:8, :]


def project_kernel(order, x_ref, p0, p1, p2, p3, squares, out_ref, stat):
    count, columns = x_ref.shape[0], p0.shape[1]
    raw = jnp.zeros((count, 32), F32)
    for k, table in enumerate((p0, p1, p2, p3)):
        here = pl.ds(pl.multiple_of(order[k] * columns, LANES), columns)
        raw = raw + lax.dot_general(
            x_ref[:, here], table[...], CONTRACT_LAST, preferred_element_type=F32
        )
    stat[:, 0:32] = raw
    out_ref[...] = stat[...].T[0:32, :]
    out_ref[24:25, :] = squares[0:1, :]


def mix_in_kernel(scale, bias, s0, s1, s2, s3, x_ref, gain, token_map, send, h_ref, out_ref,
                  cols, stat, u_ref, o_buf, o_sem):
    xs = [x_ref.at[k] for k in range(NSTREAM)]
    count, columns = xs[0].shape
    total = s0[...] + s1[...] + s2[...] + s3[...]
    rscale = lax.rsqrt(total[24:25, :] * (1.0 / (NSTREAM * D)) + EPSILON)
    logits = [scale[0] * (total[k : k + 1, :] * rscale) + bias[k] for k in range(NSTREAM)]
    pre = jax.nn.sigmoid(jnp.concatenate(logits + logits, axis=0))
    cols[:, 0:8] = pre.T

    def rows(block, carry):
        here = pl.ds(pl.multiple_of(block * ROWS, ROWS), ROWS)
        weight = [jnp.broadcast_to(cols[here, k : k + 1], (ROWS, LANES)) for k in range(NSTREAM)]
        sums = [jnp.zeros((ROWS, LANES), F32) for _ in range(NSTREAM + 1)]
        for start in range(0, columns, LANES):
            span = slice(start, start + LANES)
            value = [x[here, span].astype(F32) for x in xs]
            h = weight[0] * value[0]
            for k in range(1, NSTREAM):
                h = h + weight[k] * value[k]
            for k in range(NSTREAM):
                sums[k] = sums[k] + h * value[k]
            sums[NSTREAM] = sums[NSTREAM] + h * h
            u_ref[here, span] = (h * gain[:, span].astype(F32)).astype(BF16)
            h_ref[here, span] = h.astype(BF16)
        for k in range(NSTREAM + 1):
            stat[here, k : k + 1] = jnp.sum(sums[k], axis=1, keepdims=True)
        return carry

    lax.fori_loop(0, count // ROWS, rows, 0)
    out_ref[...] = stat[...].T[0:8, :]
    send_chunks(send, o_buf, o_sem, columns, lambda span: jnp.dot(
        token_map[...], u_ref[:, span], preferred_element_type=F32
    ))


def send_chunks(out_ref, o_buf, o_sem, columns, product):
    copies = []
    for c in range(columns // 256):
        span = slice(c * 256, c * 256 + 256)
        o_buf[:, span] = product(span).astype(BF16)
        copies.append(pltpu.make_async_copy(o_buf.at[:, span], out_ref.at[:, span], o_sem.at[c]))
        copies[c].start()
    for copy in copies:
        copy.wait()


def cot_kernel(coef, combine, moe, q_parts, x_ref, y0, y1, y2, y3, pick0, pick1,
               send, e0, e1, e2, e3, out_ref, cols, stat, c0_ref, c1_ref):
    xs, ys, es = [x_ref.at[k] for k in range(NSTREAM)], (y0, y1, y2, y3), (e0, e1, e2, e3)
    count, columns = y0.shape
    cols[:, 0:24] = coef[...].T

    def rows(block, carry):
        here = pl.ds(pl.multiple_of(block * ROWS, ROWS), ROWS)

        def column(k):
            return jnp.broadcast_to(cols[here, k : k + 1], (ROWS, LANES))

        post = [column(k) for k in range(NSTREAM)]
        first = jnp.broadcast_to(combine[here, 0:1], (ROWS, LANES))
        second = jnp.broadcast_to(combine[here, 1:2], (ROWS, LANES))
        sums = [jnp.zeros((ROWS, LANES), F32) for _ in range(20)]
        for start in range(0, columns, LANES):
            span = slice(start, start + LANES)
            dy = [y[here, span].astype(F32) for y in ys]
            value = [x[here, span].astype(F32) for x in xs]
            out = moe[here, span].astype(F32)
            d_moe = post[0] * dy[0]
            for k in range(1, NSTREAM):
                d_moe = d_moe + post[k] * dy[k]
            c0_ref[here, span] = (first * d_moe).astype(BF16)
            c1_ref[here, span] = (second * d_moe).astype(BF16)
            for i in range(NSTREAM):
                sums[i] = sums[i] + dy[i] * out
                for j in range(NSTREAM):
                    sums[4 + 4 * i + j] = sums[4 + 4 * i + j] + dy[i] * value[j]
        for k in range(20):
            stat[here, k : k + 1] = jnp.sum(sums[k], axis=1, keepdims=True)
        mix = [column(4 + k) for k in range(16)]
        for start in range(0, columns, LANES):
            span = slice(start, start + LANES)
            dy = [y[here, span].astype(F32) for y in ys]
            for i in range(NSTREAM):
                total = mix[i] * dy[0]
                for j in range(1, NSTREAM):
                    total = total + mix[4 * j + i] * dy[j]
                es[i][here, span] = total.astype(BF16)
        return carry

    lax.fori_loop(0, count // ROWS, rows, 0)
    out_ref[...] = stat[...].T[0:24, :]
    for start in range(0, columns, 256):
        span = slice(start, start + 256)
        total = jnp.dot(pick0[...], c0_ref[:, span], preferred_element_type=F32)
        total = total + jnp.dot(pick1[...], c1_ref[:, span], preferred_element_type=F32)
        send[:, span] = total.astype(BF16)
    token_map = pick0[...] + pick1[...]
    send[:, columns : columns + LANES] = jnp.dot(
        token_map, q_parts[...], preferred_element_type=F32
    ).astype(BF16)


def product_kernel(order, *refs):
    *pieces, w_ref, out_ref, rows_ref = refs
    rows = pieces[0].shape[0]

    @pl.when(pl.program_id(0) == 0)
    def join():
        for k, piece in enumerate(pieces):
            here = pl.ds(pl.multiple_of(order[k] * rows, rows), rows)
            rows_ref[here, :] = piece[...]

    total = lax.dot_general(rows_ref[...], w_ref[...], CONTRACT_LAST, preferred_element_type=F32)
    out_ref[...] = total.astype(BF16)


def product(order, pieces, weights, name):
    rows, depth = pieces[0].shape
    columns = weights.shape[0]
    whole_piece = pl.BlockSpec((rows, depth), lambda j: (0, 0))
    return pl.pallas_call(
        product_kernel,
        out_shape=sds((rows * len(pieces), columns), BF16),
        grid=(columns // 256,),
        in_specs=[pl.BlockSpec(memory_space=pltpu.SMEM)] + [whole_piece] * len(pieces)
        + [pl.BlockSpec((256, depth), lambda j: (j, 0))],
        out_specs=pl.BlockSpec((rows * len(pieces), 256), lambda j: (0, j)),
        scratch_shapes=[pltpu.VMEM((rows * len(pieces), depth), BF16)],
        compiler_params=pltpu.CompilerParams(vmem_limit_bytes=VMEM_LIMIT),
        cost_estimate=pl.CostEstimate(
            flops=2 * rows * len(pieces) * depth * columns,
            bytes_accessed=2 * columns * depth + 4 * rows * len(pieces) * columns,
            transcendentals=0,
        ),
        name=name,
    )(order, *pieces, weights)


def hidden_kernel(tail, both, z_ref, out_ref):
    count, width = both.shape[0], z_ref.shape[2]

    def rows(block, carry):
        here = pl.ds(pl.multiple_of(block * ROWS, ROWS), ROWS)
        parts = tail[here, :].astype(F32)
        q = jnp.broadcast_to(parts[:, 0:1] + parts[:, 1:2] + parts[:, 2:3], (ROWS, 256))
        for col in range(0, width, 256):
            gate = both[here, col : col + 256].astype(F32) * q
            up = both[here, width + col : width + col + 256].astype(F32) * q
            dz = z_ref[0, here, col : col + 256].astype(F32)
            for k in range(1, NSTREAM):
                dz = dz + z_ref[k, here, col : col + 256].astype(F32)
            sig = jax.nn.sigmoid(gate)
            d_gate = dz * up * sig * (1.0 + gate * (1.0 - sig))
            d_up = dz * gate * sig
            out_ref[here, col : col + 256] = d_gate.astype(BF16)
            out_ref[here, width + col : width + col + 256] = d_up.astype(BF16)
        return carry

    lax.fori_loop(0, count // ROWS, rows, 0)


def collect_kernel(back, token_map_t, gain, x_ref, out_ref, gu_ref, stat):
    count, columns = gu_ref.shape
    for start in range(0, columns, 256):
        span = slice(start, start + 256)
        du = jnp.dot(token_map_t[...], back[:, span], preferred_element_type=F32)
        gu = du * gain[:, span].astype(F32)
        gu_ref[:, span] = gu
        out_ref[:, span] = gu.astype(BF16)
    stat[...] = jnp.zeros(stat.shape, F32)

    def rows(block, carry):
        here = pl.ds(pl.multiple_of(block * ROWS, ROWS), ROWS)
        sums = [jnp.zeros((ROWS, LANES), F32) for _ in range(NSTREAM)]
        for start in range(0, columns, LANES):
            span = slice(start, start + LANES)
            gu = gu_ref[here, span]
            for k in range(NSTREAM):
                sums[k] = sums[k] + gu * x_ref[k, here, span].astype(F32)
        for k in range(NSTREAM):
            rest = jnp.sum(sums[k], axis=1, keepdims=True)
            for part in range(3):
                term = rest.astype(BF16).astype(F32)
                stat[here, 3 * k + part : 3 * k + part + 1] = term
                rest = rest - term
        return carry

    lax.fori_loop(0, count // ROWS, rows, 0)
    out_ref[:, columns : columns + LANES] = stat[...].astype(BF16)


def three_parts(rest):
    parts = []
    for part in range(3):
        parts.append(rest.astype(BF16).astype(F32))
        rest = rest - parts[part]
    return parts


def final_kernel(order, small, early, x_ref, u0, u1, u2, u3, h0, h1, h2, h3,
                 e0, e1, e2, e3, p0, p1, p2, p3, out_ref,
                 cols, coef_ref, s_buf, d_buf, u_buf, h_buf, e_buf, x_buf, p_buf, o_buf,
                 s_sem, in_sem, o_sem):
    count, columns = e0.shape
    us, hs, es, ps = (u0, u1, u2, u3), (h0, h1, h2, h3), (e0, e1, e2, e3), (p0, p1, p2, p3)
    firsts = [
        pltpu.make_async_copy(small, s_buf, s_sem.at[0]),
        pltpu.make_async_copy(early, d_buf, s_sem.at[1]),
    ]
    where = [pl.ds(pl.multiple_of(order[k] * columns, LANES), columns) for k in range(4)]
    grads = [pltpu.make_async_copy(us[k], u_buf.at[k], in_sem.at[k, 0]) for k in range(4)]
    others = [
        [
            pltpu.make_async_copy(es[k], e_buf.at[k], in_sem.at[k, 1]),
            pltpu.make_async_copy(hs[k], h_buf.at[k], in_sem.at[k, 3]),
            pltpu.make_async_copy(x_ref.at[:, where[k]], x_buf.at[k], in_sem.at[k, 4]),
        ] + [
            pltpu.make_async_copy(
                ps[k], p_buf.at[k, pl.ds(32 * part, 32), :], in_sem.at[k, 5 + part]
            )
            for part in range(3)
        ]
        for k in range(4)
    ]
    for copy in firsts + grads + others[0] + others[1] + others[2] + others[3]:
        copy.start()
    for copy in firsts:
        copy.wait()
    coef_ref[...] = jnp.zeros(coef_ref.shape, F32)
    for part, term in enumerate(three_parts(d_buf[...])):
        coef_ref[32 * part : 32 * part + 24, :] = term
    coef_ref[96:120, :] = s_buf[...]
    cols[...] = coef_ref[...].T
    for copy in grads:
        copy.wait()
    sums = u_buf[0, :, columns : columns + LANES].astype(F32)
    for k in range(1, NSTREAM):
        sums = sums + u_buf[k, :, columns : columns + LANES].astype(F32)
    a_part = [
        sums[:, 3 * n : 3 * n + 1] + sums[:, 3 * n + 1 : 3 * n + 2] + sums[:, 3 * n + 2 : 3 * n + 3]
        for n in range(NSTREAM)
    ]
    pre = [cols[:, 96 + n : 97 + n] for n in range(4)]
    b_part = [cols[:, 100 + n : 101 + n] for n in range(4)]
    raw = [cols[:, 104 + n : 105 + n] for n in range(4)]
    q, r, d_rscale, scale = (cols[:, 108 + n : 109 + n] for n in range(4))
    norm_dot = pre[0] * a_part[0]
    for n in range(1, 4):
        norm_dot = norm_dot + pre[n] * a_part[n]
    cube = q * q * q * (1.0 / D) * norm_dot
    for n in range(4):
        d_pre = q * a_part[n] - cube * b_part[n]
        d_proj = d_pre * scale * pre[n] * (1.0 - pre[n])
        d_rscale = d_rscale + d_proj * raw[n]
        for part, term in enumerate(three_parts(r * d_proj)):
            cols[:, 32 * part + n : 32 * part + n + 1] = term
    own = cols[:, 112:113]
    by_u = jnp.broadcast_to(own * q, (count, 256))
    by_h = jnp.broadcast_to(-own * cube, (count, 256))
    by_x = jnp.broadcast_to(-(r * r * r) * (1.0 / (NSTREAM * D)) * d_rscale, (count, 256))
    weights = cols[:, 0:96].astype(BF16)
    outs = []
    for k in range(4):
        for copy in others[k]:
            copy.wait()
        for start in range(0, columns, 256):
            span = slice(start, start + 256)
            total = jnp.dot(weights, p_buf[k, :, span], preferred_element_type=F32)
            total = total + e_buf[k, :, span].astype(F32)
            total = total + by_u * u_buf[k, :, span].astype(F32)
            total = total + by_h * h_buf[k, :, span].astype(F32)
            total = total + by_x * x_buf[k, :, span].astype(F32)
            o_buf[k, :, span] = total.astype(BF16)
        outs.append(pltpu.make_async_copy(o_buf.at[k], out_ref.at[:, where[k]], o_sem.at[k]))
        outs[k].start()
    for copy in outs:
        copy.wait()


def slot_maps(expert_ids, experts, capacity):
    hits = (expert_ids[:, :, None] == jnp.arange(experts, dtype=jnp.int32)).astype(jnp.int32)
    per_token = jnp.sum(hits, axis=1)
    count = expert_ids.shape[0]
    before = (jnp.arange(count)[:, None] > jnp.arange(count)[None, :]).astype(BF16)
    earlier = jnp.dot(before, per_token.astype(BF16), preferred_element_type=F32).astype(jnp.int32)
    position = jnp.sum(hits * earlier[:, None, :], axis=2)
    slot_id = expert_ids * capacity + position
    slots = jnp.arange(experts * capacity, dtype=jnp.int32)
    pick = [(slot_id[None, :, k] == slots[:, None]).astype(BF16) for k in range(TOP)]
    back = jnp.any(slot_id[:, :, None] == slots[None, None, :], axis=1).astype(BF16)
    return pick, back


def reduce_rows(part, me):
    quarter = part.shape[0] // NSTREAM
    pieces = [
        lax.dynamic_slice_in_dim(part, (me + k) % NSTREAM * quarter, quarter, 0)
        for k in range(NSTREAM)
    ]
    total = pieces[0].astype(F32)
    for k in range(1, NSTREAM):
        total = total + shift(pieces[k], k).astype(F32)
    return total.astype(BF16)


def shards(streams, cotangent, moe_out, coef_proj, coef_scale, coef_bias, norm_gain, expert_ids,
           combine, w_gate, w_up, w_down):
    me = lax.axis_index("stream")
    count, columns = moe_out.shape
    experts = lax.axis_size("expert") // 2
    capacity = max(2, 2 * count * TOP // experts)
    order = ((me - jnp.arange(NSTREAM, dtype=jnp.int32)) % NSTREAM).astype(jnp.int32)

    table = jnp.pad(coef_proj, ((0, 0), (0, 32 - coef_proj.shape[1]), (0, 0)))

    def table_for(k):
        return lax.dynamic_index_in_dim(table, (me + k) % NSTREAM, 0, False)

    tables = [table_for(0)] + [shift(table_for(k), k) for k in range(1, NSTREAM)]

    x_flat = streams.reshape(count, NSTREAM * columns)
    x_send = jnp.stack([x_flat[:, k * columns : (k + 1) * columns] for k in range(NSTREAM)])
    x_all = lax.all_to_all(x_send, "stream", split_axis=0, concat_axis=0, tiled=True)

    scratch = pltpu.VMEM((count, LANES), F32)
    squares = call(
        squares_kernel, "squares", sds((8, count), F32), [x_flat], [scratch],
        2 * count * NSTREAM * columns,
    )
    sums = call(
        project_kernel, "project", sds((32, count), F32), [order, x_flat] + tables + [squares],
        [scratch], 2 * count * 32 * NSTREAM * columns, smem=1,
    )
    y_flat, sums = lax.optimization_barrier((cotangent.reshape(count, -1), sums))
    partial_sums = spread(sums)
    pick, back_map = slot_maps(expert_ids, experts, capacity)
    slots = experts * capacity
    chunks = columns // 256
    dma = pltpu.SemaphoreType.DMA
    send_u, h_own, in_sums = call(
        mix_in_kernel, "mix_in",
        [sds((slots, columns), BF16), sds((count, columns), BF16), sds((8, count), F32)],
        [coef_scale, coef_bias] + partial_sums + [x_all, norm_gain[None, :], pick[0] + pick[1]],
        [
            scratch, scratch, pltpu.VMEM((count, columns), BF16),
            pltpu.VMEM((slots, columns), BF16), dma((chunks,)),
        ],
        2 * slots * count * columns, smem=2, hbm_outs=1,
    )
    *partial_sums, in_sums = lax.optimization_barrier((*partial_sums, in_sums))
    sums = partial_sums[0] + partial_sums[1] + partial_sums[2] + partial_sums[3]
    projected, squares = sums[0:24], sums[24]
    rscale = lax.rsqrt(squares / (NSTREAM * D) + EPSILON)
    projection = projected * rscale[None, :]
    in_sums, projection = lax.optimization_barrier((in_sums, projection))
    pre = jax.nn.sigmoid(coef_scale[0] * projection[0:4] + coef_bias[0:4, None])
    def to_experts(array):
        blocks = array.reshape(2 * experts, slots // (2 * experts), array.shape[1])
        moved = lax.all_to_all(blocks, "expert", split_axis=0, concat_axis=0, tiled=True)
        return moved.reshape(array.shape)

    rows_u = to_experts(send_u)

    swap = [(i, i ^ 1) for i in range(2 * experts)]

    def sibling(array):
        return lax.ppermute(array, "expert", swap)

    w_both = jnp.concatenate([w_gate, sibling(w_gate), w_up, sibling(w_up)], axis=1)
    wide = columns + LANES
    w_hidden = jnp.concatenate([w_down, sibling(w_down)], axis=0)
    w_hidden = jnp.pad(w_hidden, ((0, 0), (0, LANES)))

    y_own = [
        lax.dynamic_slice_in_dim(y_flat, (me + k) % NSTREAM * columns, columns, 1)
        for k in range(NSTREAM)
    ]
    *y_own, in_sums = lax.optimization_barrier((*y_own, in_sums))
    y_rel = [y_own[0]] + [shift(y_own[k], k) for k in range(1, NSTREAM)]

    in_sums = small_sum(in_sums)
    b_part, square_sum = in_sums[0:4], in_sums[4]
    qscale = lax.rsqrt(square_sum / D + EPSILON)
    q_high = qscale.astype(BF16)
    q_rest = qscale - q_high.astype(F32)
    q_mid = q_rest.astype(BF16)
    q_low = (q_rest - q_mid.astype(F32)).astype(BF16)
    q_parts = jnp.pad(jnp.stack([q_high, q_mid, q_low], axis=1), ((0, 0), (0, LANES - 3)))

    def later(values):
        post = 2.0 * jax.nn.sigmoid(coef_scale[1] * values[4:8] + coef_bias[4:8, None])
        return post, sinkhorn(coef_scale[2] * values[8:] + coef_bias[8:, None])

    (post, mixing), pullback = jax.vjp(later, projection)
    mix_rel = relative(relative(mixing, me, 0), me, 1).reshape(16, count)
    coef = jnp.concatenate([relative(post, me), mix_rel, jnp.zeros((4, count), F32)])
    half = pltpu.VMEM((count, columns), BF16)
    piece = sds((count, columns), BF16)
    moe_out, w_both, w_hidden = lax.optimization_barrier((moe_out, w_both, w_hidden))
    send_c, *grad_mix, cot_sums = call(
        cot_kernel, "cot",
        [sds((slots, wide), BF16), piece, piece, piece, piece, sds((24, count), F32)],
        [coef, combine, moe_out, q_parts, x_all] + y_rel + pick,
        [scratch, scratch, half, half],
        4 * slots * count * columns,
    )
    rows_c = to_experts(send_c)
    h_own, *_ = lax.optimization_barrier((h_own, y_rel[1], y_rel[2], y_rel[3]))
    h_rel = [h_own, shift(h_own, 1), None, shift(h_own, 3)]

    part_both = jnp.dot(rows_u, w_both, preferred_element_type=F32).astype(BF16)
    both = reduce_rows(part_both, me)
    rows_c, both, h_rel[1], h_rel[3] = lax.optimization_barrier((rows_c, both, h_rel[1], h_rel[3]))
    none = jnp.zeros((1,), jnp.int32)
    part_hidden = product(none, [rows_c], w_hidden, "hidden_product")
    quarter = slots // NSTREAM
    hidden = part_hidden.reshape(NSTREAM, quarter, -1)
    hidden = lax.all_to_all(hidden, "stream", split_axis=0, concat_axis=0, tiled=True)
    tail = lax.dynamic_slice(rows_c, (me * quarter, columns), (quarter, LANES))
    d_both = call(hidden_kernel, "hidden", sds(both.shape, BF16), [tail, both, hidden], limit=16)
    d_both = spread(d_both)
    part_du = product(order, d_both, w_both, "input_product")
    back = to_experts(part_du)

    *grad_mix, h_own, _, _, _, _ = lax.optimization_barrier((*grad_mix, h_own, *d_both))
    h_rel[2] = shift(h_own, 2)
    e_rel = [grad_mix[0]] + [shift(grad_mix[(4 - k) % 4], k) for k in range(1, NSTREAM)]
    post_dots = relative(cot_sums[0:4], me)
    mix_dots = relative(cot_sums[4:20].reshape(NSTREAM, NSTREAM, count), me).reshape(16, count)
    cot_sums = small_sum(jnp.concatenate([post_dots, mix_dots, jnp.zeros((4, count), F32)]))
    (d_proj,) = pullback((cot_sums[0:4], cot_sums[4:20].reshape(NSTREAM, NSTREAM, count)))
    early_rscale = jnp.sum(d_proj * projected, axis=0)
    early = rscale[None, :] * d_proj
    small = jnp.concatenate(
        [pre, b_part, projected[0:4], qscale[None], rscale[None], early_rscale[None],
         jnp.broadcast_to(coef_scale[0:1, None], (1, count)),
         lax.dynamic_slice_in_dim(pre, me, 1, 0), jnp.zeros((7, count), F32)]
    )
    back, h_rel[2], *e_rel = lax.optimization_barrier((back, h_rel[2], *e_rel))
    gu_own = call(
        collect_kernel, "collect", sds((count, wide), BF16),
        [back, back_map, norm_gain[None, :], x_all],
        [pltpu.VMEM((count, columns), F32), scratch],
        2 * slots * count * columns, limit=20,
    )
    gu_rel = spread(gu_own)
    four = pltpu.VMEM((NSTREAM, count, columns), BF16)
    grads = call(
        final_kernel, "final", sds((count, NSTREAM * columns), BF16),
        [order, small, early, x_flat] + gu_rel + h_rel + e_rel + tables,
        [
            scratch, pltpu.VMEM((LANES, count), F32), pltpu.VMEM((24, count), F32),
            pltpu.VMEM((24, count), F32), pltpu.VMEM((NSTREAM, count, wide), BF16), four, four, four,
            pltpu.VMEM((NSTREAM, 96, columns), BF16), four,
            dma((2,)), dma((NSTREAM, 8)), dma((NSTREAM,)),
        ],
        2 * count * 96 * NSTREAM * columns, smem=1, anywhere=True,
    )
    return grads.reshape(streams.shape)


def solution(mesh):
    placed = (
        P("expert", "stream", None),
        P("expert", "stream", None),
        P("expert", "stream"),
        P(None, None, "stream"),
        P(),
        P(),
        P("stream"),
        P("expert", None),
        P("expert", None),
        P("stream", "expert"),
        P("stream", "expert"),
        P("expert", "stream"),
    )
    return jax.shard_map(
        shards, mesh=mesh, in_specs=placed, out_specs=P("expert", "stream", None), check_vma=False
    )
```

```python
import jax
import jax.numpy as jnp
from jax import lax
from jax.experimental import pallas as pl
from jax.experimental.pallas import tpu as pltpu
from jax.sharding import PartitionSpec as P

D = 7168
NSTREAM = 4
SINK = 4
TOP = 2
EPSILON = 1e-06
F32 = jnp.float32
BF16 = jnp.bfloat16
ROWS = 16
LANES = 128
VMEM_LIMIT = 60 * 1024 * 1024
CONTRACT_LAST = (((1,), (1,)), ((), ()))


def sinkhorn(logits):
    mixing = jnp.exp(logits).reshape(NSTREAM, NSTREAM, -1)
    for iteration in range(SINK):
        mixing = mixing / jnp.sum(mixing, axis=1, keepdims=True)
        mixing = mixing / jnp.sum(mixing, axis=0, keepdims=True)
    return mixing


def relative(array, me, axis=0):
    flipped = jnp.flip(array, axis)
    doubled = jnp.concatenate([flipped, flipped], axis)
    return lax.dynamic_slice_in_dim(doubled, NSTREAM - 1 - me, NSTREAM, axis)


def shift(array, step):
    pairs = [(i, (i + step) % NSTREAM) for i in range(NSTREAM)]
    return lax.ppermute(array, "stream", pairs)


def small_sum(array):
    return array + shift(array, 1) + shift(array, 2) + shift(array, 3)


def spread(array):
    return [array, shift(array, 1), shift(array, 2), shift(array, 3)]


def whole(count):
    return [pl.BlockSpec(memory_space=pltpu.VMEM)] * count


def call(kernel, name, out_shape, args, scratch=(), flops=0, smem=0, anywhere=False, hbm_outs=0, limit=60):
    single = not isinstance(out_shape, (list, tuple))
    outs = [out_shape] if single else list(out_shape)
    moved = sum(a.size * a.dtype.itemsize for a in list(args) + outs)
    place = [pl.BlockSpec(memory_space=pl.ANY)] if anywhere else whole(1)
    specs = [pl.BlockSpec(memory_space=pltpu.SMEM)] * smem + place * (len(args) - smem)
    out_place = [pl.BlockSpec(memory_space=pl.ANY)] * hbm_outs + place * (len(outs) - hbm_outs)
    return pl.pallas_call(
        kernel,
        out_shape=out_shape,
        in_specs=specs,
        out_specs=out_place[0] if single else out_place,
        scratch_shapes=list(scratch),
        compiler_params=pltpu.CompilerParams(vmem_limit_bytes=limit * 1024 * 1024),
        cost_estimate=pl.CostEstimate(flops=flops, bytes_accessed=moved, transcendentals=0),
        name=name,
    )(*args)


def sds(shape, dtype):
    return jax.ShapeDtypeStruct(shape, dtype)


def squares_kernel(x_ref, out_ref, stat):
    def rows(block, carry):
        here = pl.ds(pl.multiple_of(block * ROWS, ROWS), ROWS)
        total = jnp.zeros((ROWS, LANES), F32)
        for start in range(0, x_ref.shape[1], LANES):
            value = x_ref[here, start : start + LANES].astype(F32)
            total = total + value * value
        stat[here, 0:1] = jnp.sum(total, axis=1, keepdims=True)
        return carry

    lax.fori_loop(0, x_ref.shape[0] // ROWS, rows, 0)
    out_ref[...] = stat[...].T[0:8, :]


def project_kernel(order, x_ref, p0, p1, p2, p3, squares, out_ref, stat):
    count, columns = x_ref.shape[0], p0.shape[1]
    raw = jnp.zeros((count, 32), F32)
    for k, table in enumerate((p0, p1, p2, p3)):
        here = pl.ds(pl.multiple_of(order[k] * columns, LANES), columns)
        raw = raw + lax.dot_general(
            x_ref[:, here], table[...], CONTRACT_LAST, preferred_element_type=F32
        )
    stat[:, 0:32] = raw
    out_ref[...] = stat[...].T[0:32, :]
    out_ref[24:25, :] = squares[0:1, :]


def mix_in_kernel(scale, bias, s0, s1, s2, s3, x_ref, gain, token_map, send, h_ref, out_ref,
                  cols, stat, u_ref, o_buf, o_sem):
    xs = [x_ref.at[k] for k in range(NSTREAM)]
    count, columns = xs[0].shape
    total = s0[...] + s1[...] + s2[...] + s3[...]
    rscale = lax.rsqrt(total[24:25, :] * (1.0 / (NSTREAM * D)) + EPSILON)
    logits = [scale[0] * (total[k : k + 1, :] * rscale) + bias[k] for k in range(NSTREAM)]
    pre = jax.nn.sigmoid(jnp.concatenate(logits + logits, axis=0))
    cols[:, 0:8] = pre.T

    def rows(block, carry):
        here = pl.ds(pl.multiple_of(block * ROWS, ROWS), ROWS)
        weight = [jnp.broadcast_to(cols[here, k : k + 1], (ROWS, LANES)) for k in range(NSTREAM)]
        sums = [jnp.zeros((ROWS, LANES), F32) for _ in range(NSTREAM + 1)]
        for start in range(0, columns, LANES):
            span = slice(start, start + LANES)
            value = [x[here, span].astype(F32) for x in xs]
            h = weight[0] * value[0]
            for k in range(1, NSTREAM):
                h = h + weight[k] * value[k]
            for k in range(NSTREAM):
                sums[k] = sums[k] + h * value[k]
            sums[NSTREAM] = sums[NSTREAM] + h * h
            u_ref[here, span] = (h * gain[:, span].astype(F32)).astype(BF16)
            h_ref[here, span] = h.astype(BF16)
        for k in range(NSTREAM + 1):
            stat[here, k : k + 1] = jnp.sum(sums[k], axis=1, keepdims=True)
        return carry

    lax.fori_loop(0, count // ROWS, rows, 0)
    out_ref[...] = stat[...].T[0:8, :]
    send_chunks(send, o_buf, o_sem, columns, lambda span: jnp.dot(
        token_map[...], u_ref[:, span], preferred_element_type=F32
    ))


def send_chunks(out_ref, o_buf, o_sem, columns, product):
    copies = []
    for c in range(columns // 256):
        span = slice(c * 256, c * 256 + 256)
        o_buf[:, span] = product(span).astype(BF16)
        copies.append(pltpu.make_async_copy(o_buf.at[:, span], out_ref.at[:, span], o_sem.at[c]))
        copies[c].start()
    for copy in copies:
        copy.wait()


def cot_kernel(coef, combine, moe, q_parts, x_ref, y0, y1, y2, y3, pick0, pick1,
               send, e0, e1, e2, e3, out_ref, cols, stat, c0_ref, c1_ref):
    xs, ys, es = [x_ref.at[k] for k in range(NSTREAM)], (y0, y1, y2, y3), (e0, e1, e2, e3)
    count, columns = y0.shape
    cols[:, 0:24] = coef[...].T

    def rows(block, carry):
        here = pl.ds(pl.multiple_of(block * ROWS, ROWS), ROWS)

        def column(k):
            return jnp.broadcast_to(cols[here, k : k + 1], (ROWS, LANES))

        post = [column(k) for k in range(NSTREAM)]
        first = jnp.broadcast_to(combine[here, 0:1], (ROWS, LANES))
        second = jnp.broadcast_to(combine[here, 1:2], (ROWS, LANES))
        sums = [jnp.zeros((ROWS, LANES), F32) for _ in range(20)]
        for start in range(0, columns, LANES):
            span = slice(start, start + LANES)
            dy = [y[here, span].astype(F32) for y in ys]
            value = [x[here, span].astype(F32) for x in xs]
            out = moe[here, span].astype(F32)
            d_moe = post[0] * dy[0]
            for k in range(1, NSTREAM):
                d_moe = d_moe + post[k] * dy[k]
            c0_ref[here, span] = (first * d_moe).astype(BF16)
            c1_ref[here, span] = (second * d_moe).astype(BF16)
            for i in range(NSTREAM):
                sums[i] = sums[i] + dy[i] * out
                for j in range(NSTREAM):
                    sums[4 + 4 * i + j] = sums[4 + 4 * i + j] + dy[i] * value[j]
        for k in range(20):
            stat[here, k : k + 1] = jnp.sum(sums[k], axis=1, keepdims=True)
        mix = [column(4 + k) for k in range(16)]
        for start in range(0, columns, LANES):
            span = slice(start, start + LANES)
            dy = [y[here, span].astype(F32) for y in ys]
            for i in range(NSTREAM):
                total = mix[i] * dy[0]
                for j in range(1, NSTREAM):
                    total = total + mix[4 * j + i] * dy[j]
                es[i][here, span] = total.astype(BF16)
        return carry

    lax.fori_loop(0, count // ROWS, rows, 0)
    out_ref[...] = stat[...].T[0:24, :]
    for start in range(0, columns, 256):
        span = slice(start, start + 256)
        total = jnp.dot(pick0[...], c0_ref[:, span], preferred_element_type=F32)
        total = total + jnp.dot(pick1[...], c1_ref[:, span], preferred_element_type=F32)
        send[:, span] = total.astype(BF16)
    token_map = pick0[...] + pick1[...]
    send[:, columns : columns + LANES] = jnp.dot(
        token_map, q_parts[...], preferred_element_type=F32
    ).astype(BF16)


def product_kernel(order, *refs):
    *pieces, w_ref, out_ref, rows_ref = refs
    rows = pieces[0].shape[0]

    @pl.when(pl.program_id(0) == 0)
    def join():
        for k, piece in enumerate(pieces):
            here = pl.ds(pl.multiple_of(order[k] * rows, rows), rows)
            rows_ref[here, :] = piece[...]

    total = lax.dot_general(rows_ref[...], w_ref[...], CONTRACT_LAST, preferred_element_type=F32)
    out_ref[...] = total.astype(BF16)


def product(order, pieces, weights, name):
    rows, depth = pieces[0].shape
    columns = weights.shape[0]
    whole_piece = pl.BlockSpec((rows, depth), lambda j: (0, 0))
    return pl.pallas_call(
        product_kernel,
        out_shape=sds((rows * len(pieces), columns), BF16),
        grid=(columns // 256,),
        in_specs=[pl.BlockSpec(memory_space=pltpu.SMEM)] + [whole_piece] * len(pieces)
        + [pl.BlockSpec((256, depth), lambda j: (j, 0))],
        out_specs=pl.BlockSpec((rows * len(pieces), 256), lambda j: (0, j)),
        scratch_shapes=[pltpu.VMEM((rows * len(pieces), depth), BF16)],
        compiler_params=pltpu.CompilerParams(vmem_limit_bytes=VMEM_LIMIT),
        cost_estimate=pl.CostEstimate(
            flops=2 * rows * len(pieces) * depth * columns,
            bytes_accessed=2 * columns * depth + 4 * rows * len(pieces) * columns,
            transcendentals=0,
        ),
        name=name,
    )(order, *pieces, weights)


def hidden_kernel(tail, both, z_ref, out_ref):
    count, width = both.shape[0], z_ref.shape[2]

    def rows(block, carry):
        here = pl.ds(pl.multiple_of(block * ROWS, ROWS), ROWS)
        parts = tail[here, :].astype(F32)
        q = jnp.broadcast_to(parts[:, 0:1] + parts[:, 1:2] + parts[:, 2:3], (ROWS, 256))
        for col in range(0, width, 256):
            gate = both[here, col : col + 256].astype(F32) * q
            up = both[here, width + col : width + col + 256].astype(F32) * q
            dz = z_ref[0, here, col : col + 256].astype(F32)
            for k in range(1, NSTREAM):
                dz = dz + z_ref[k, here, col : col + 256].astype(F32)
            sig = jax.nn.sigmoid(gate)
            d_gate = dz * up * sig * (1.0 + gate * (1.0 - sig))
            d_up = dz * gate * sig
            out_ref[here, col : col + 256] = d_gate.astype(BF16)
            out_ref[here, width + col : width + col + 256] = d_up.astype(BF16)
        return carry

    lax.fori_loop(0, count // ROWS, rows, 0)


def collect_kernel(back, token_map_t, gain, x_ref, out_ref, gu_ref, stat):
    count, columns = gu_ref.shape
    for start in range(0, columns, 256):
        span = slice(start, start + 256)
        du = jnp.dot(token_map_t[...], back[:, span], preferred_element_type=F32)
        gu = du * gain[:, span].astype(F32)
        gu_ref[:, span] = gu
        out_ref[:, span] = gu.astype(BF16)
    stat[...] = jnp.zeros(stat.shape, F32)

    def rows(block, carry):
        here = pl.ds(pl.multiple_of(block * ROWS, ROWS), ROWS)
        sums = [jnp.zeros((ROWS, LANES), F32) for _ in range(NSTREAM)]
        for start in range(0, columns, LANES):
            span = slice(start, start + LANES)
            gu = gu_ref[here, span]
            for k in range(NSTREAM):
                sums[k] = sums[k] + gu * x_ref[k, here, span].astype(F32)
        for k in range(NSTREAM):
            rest = jnp.sum(sums[k], axis=1, keepdims=True)
            for part in range(3):
                term = rest.astype(BF16).astype(F32)
                stat[here, 3 * k + part : 3 * k + part + 1] = term
                rest = rest - term
        return carry

    lax.fori_loop(0, count // ROWS, rows, 0)
    out_ref[:, columns : columns + LANES] = stat[...].astype(BF16)


def three_parts(rest):
    parts = []
    for part in range(3):
        parts.append(rest.astype(BF16).astype(F32))
        rest = rest - parts[part]
    return parts


def final_kernel(order, small, early, x_ref, u0, u1, u2, u3, h0, h1, h2, h3,
                 e0, e1, e2, e3, p0, p1, p2, p3, out_ref,
                 cols, coef_ref, s_buf, d_buf, u_buf, h_buf, e_buf, x_buf, p_buf, o_buf,
                 s_sem, in_sem, o_sem):
    count, columns = e0.shape
    us, hs, es, ps = (u0, u1, u2, u3), (h0, h1, h2, h3), (e0, e1, e2, e3), (p0, p1, p2, p3)
    firsts = [
        pltpu.make_async_copy(small, s_buf, s_sem.at[0]),
        pltpu.make_async_copy(early, d_buf, s_sem.at[1]),
    ]
    where = [pl.ds(pl.multiple_of(order[k] * columns, LANES), columns) for k in range(4)]
    grads = [pltpu.make_async_copy(us[k], u_buf.at[k], in_sem.at[k, 0]) for k in range(4)]
    others = [
        [
            pltpu.make_async_copy(es[k], e_buf.at[k], in_sem.at[k, 1]),
            pltpu.make_async_copy(hs[k], h_buf.at[k], in_sem.at[k, 3]),
            pltpu.make_async_copy(x_ref.at[:, where[k]], x_buf.at[k], in_sem.at[k, 4]),
        ] + [
            pltpu.make_async_copy(
                ps[k], p_buf.at[k, pl.ds(32 * part, 32), :], in_sem.at[k, 5 + part]
            )
            for part in range(3)
        ]
        for k in range(4)
    ]
    for copy in firsts + grads + others[0] + others[1] + others[2] + others[3]:
        copy.start()
    for copy in firsts:
        copy.wait()
    coef_ref[...] = jnp.zeros(coef_ref.shape, F32)
    for part, term in enumerate(three_parts(d_buf[...])):
        coef_ref[32 * part : 32 * part + 24, :] = term
    coef_ref[96:120, :] = s_buf[...]
    cols[...] = coef_ref[...].T
    for copy in grads:
        copy.wait()
    sums = u_buf[0, :, columns : columns + LANES].astype(F32)
    for k in range(1, NSTREAM):
        sums = sums + u_buf[k, :, columns : columns + LANES].astype(F32)
    a_part = [
        sums[:, 3 * n : 3 * n + 1] + sums[:, 3 * n + 1 : 3 * n + 2] + sums[:, 3 * n + 2 : 3 * n + 3]
        for n in range(NSTREAM)
    ]
    pre = [cols[:, 96 + n : 97 + n] for n in range(4)]
    b_part = [cols[:, 100 + n : 101 + n] for n in range(4)]
    raw = [cols[:, 104 + n : 105 + n] for n in range(4)]
    q, r, d_rscale, scale = (cols[:, 108 + n : 109 + n] for n in range(4))
    norm_dot = pre[0] * a_part[0]
    for n in range(1, 4):
        norm_dot = norm_dot + pre[n] * a_part[n]
    cube = q * q * q * (1.0 / D) * norm_dot
    for n in range(4):
        d_pre = q * a_part[n] - cube * b_part[n]
        d_proj = d_pre * scale * pre[n] * (1.0 - pre[n])
        d_rscale = d_rscale + d_proj * raw[n]
        for part, term in enumerate(three_parts(r * d_proj)):
            cols[:, 32 * part + n : 32 * part + n + 1] = term
    own = cols[:, 112:113]
    by_u = jnp.broadcast_to(own * q, (count, 256))
    by_h = jnp.broadcast_to(-own * cube, (count, 256))
    by_x = jnp.broadcast_to(-(r * r * r) * (1.0 / (NSTREAM * D)) * d_rscale, (count, 256))
    weights = cols[:, 0:96].astype(BF16)
    outs = []
    for k in range(4):
        for copy in others[k]:
            copy.wait()
        for start in range(0, columns, 256):
            span = slice(start, start + 256)
            total = jnp.dot(weights, p_buf[k, :, span], preferred_element_type=F32)
            total = total + e_buf[k, :, span].astype(F32)
            total = total + by_u * u_buf[k, :, span].astype(F32)
            total = total + by_h * h_buf[k, :, span].astype(F32)
            total = total + by_x * x_buf[k, :, span].astype(F32)
            o_buf[k, :, span] = total.astype(BF16)
        outs.append(pltpu.make_async_copy(o_buf.at[k], out_ref.at[:, where[k]], o_sem.at[k]))
        outs[k].start()
    for copy in outs:
        copy.wait()


def slot_maps(expert_ids, experts, capacity):
    hits = (expert_ids[:, :, None] == jnp.arange(experts, dtype=jnp.int32)).astype(jnp.int32)
    per_token = jnp.sum(hits, axis=1)
    count = expert_ids.shape[0]
    before = (jnp.arange(count)[:, None] > jnp.arange(count)[None, :]).astype(BF16)
    earlier = jnp.dot(before, per_token.astype(BF16), preferred_element_type=F32).astype(jnp.int32)
    position = jnp.sum(hits * earlier[:, None, :], axis=2)
    slot_id = expert_ids * capacity + position
    slots = jnp.arange(experts * capacity, dtype=jnp.int32)
    pick = [(slot_id[None, :, k] == slots[:, None]).astype(BF16) for k in range(TOP)]
    back = jnp.any(slot_id[:, :, None] == slots[None, None, :], axis=1).astype(BF16)
    return pick, back


def reduce_rows(part, me):
    quarter = part.shape[0] // NSTREAM
    pieces = [
        lax.dynamic_slice_in_dim(part, (me + k) % NSTREAM * quarter, quarter, 0)
        for k in range(NSTREAM)
    ]
    total = pieces[0].astype(F32)
    for k in range(1, NSTREAM):
        total = total + shift(pieces[k], k).astype(F32)
    return total.astype(BF16)


def shards(streams, cotangent, moe_out, coef_proj, coef_scale, coef_bias, norm_gain, expert_ids,
           combine, w_gate, w_up, w_down):
    me = lax.axis_index("stream")
    count, columns = moe_out.shape
    experts = lax.axis_size("expert") // 2
    capacity = max(2, 2 * count * TOP // experts)
    order = ((me - jnp.arange(NSTREAM, dtype=jnp.int32)) % NSTREAM).astype(jnp.int32)

    x_flat = streams.reshape(count, NSTREAM * columns)
    x_send = jnp.stack([x_flat[:, k * columns : (k + 1) * columns] for k in range(NSTREAM)])
    coef_proj, x_send = lax.optimization_barrier((coef_proj, x_send))
    x_all = lax.all_to_all(x_send, "stream", split_axis=0, concat_axis=0, tiled=True)

    table = jnp.pad(coef_proj, ((0, 0), (0, 32 - coef_proj.shape[1]), (0, 0)))

    def table_for(k):
        return lax.dynamic_index_in_dim(table, (me + k) % NSTREAM, 0, False)

    tables = [table_for(0)] + [shift(table_for(k), k) for k in range(1, NSTREAM)]

    scratch = pltpu.VMEM((count, LANES), F32)
    squares = call(
        squares_kernel, "squares", sds((8, count), F32), [x_flat], [scratch],
        2 * count * NSTREAM * columns,
    )
    sums = call(
        project_kernel, "project", sds((32, count), F32), [order, x_flat] + tables + [squares],
        [scratch], 2 * count * 32 * NSTREAM * columns, smem=1,
    )
    y_flat, sums = lax.optimization_barrier((cotangent.reshape(count, -1), sums))
    partial_sums = spread(sums)
    pick, back_map = slot_maps(expert_ids, experts, capacity)
    slots = experts * capacity
    chunks = columns // 256
    dma = pltpu.SemaphoreType.DMA
    send_u, h_own, in_sums = call(
        mix_in_kernel, "mix_in",
        [sds((slots, columns), BF16), sds((count, columns), BF16), sds((8, count), F32)],
        [coef_scale, coef_bias] + partial_sums + [x_all, norm_gain[None, :], pick[0] + pick[1]],
        [
            scratch, scratch, pltpu.VMEM((count, columns), BF16),
            pltpu.VMEM((slots, columns), BF16), dma((chunks,)),
        ],
        2 * slots * count * columns, smem=2, hbm_outs=1,
    )
    *partial_sums, in_sums = lax.optimization_barrier((*partial_sums, in_sums))
    sums = partial_sums[0] + partial_sums[1] + partial_sums[2] + partial_sums[3]
    projected, squares = sums[0:24], sums[24]
    rscale = lax.rsqrt(squares / (NSTREAM * D) + EPSILON)
    projection = projected * rscale[None, :]
    in_sums, projection = lax.optimization_barrier((in_sums, projection))
    pre = jax.nn.sigmoid(coef_scale[0] * projection[0:4] + coef_bias[0:4, None])
    def to_experts(array):
        blocks = array.reshape(2 * experts, slots // (2 * experts), array.shape[1])
        moved = lax.all_to_all(blocks, "expert", split_axis=0, concat_axis=0, tiled=True)
        return moved.reshape(array.shape)

    rows_u = to_experts(send_u)

    swap = [(i, i ^ 1) for i in range(2 * experts)]

    def sibling(array):
        return lax.ppermute(array, "expert", swap)

    w_both = jnp.concatenate([w_gate, sibling(w_gate), w_up, sibling(w_up)], axis=1)
    wide = columns + LANES
    w_hidden = jnp.concatenate([w_down, sibling(w_down)], axis=0)
    w_hidden = jnp.pad(w_hidden, ((0, 0), (0, LANES)))

    y_own = [
        lax.dynamic_slice_in_dim(y_flat, (me + k) % NSTREAM * columns, columns, 1)
        for k in range(NSTREAM)
    ]
    *y_own, in_sums = lax.optimization_barrier((*y_own, in_sums))
    y_rel = [y_own[0]] + [shift(y_own[k], k) for k in range(1, NSTREAM)]

    in_sums, y_rel[1] = lax.optimization_barrier((in_sums, y_rel[1]))
    in_sums = small_sum(in_sums)
    b_part, square_sum = in_sums[0:4], in_sums[4]
    qscale = lax.rsqrt(square_sum / D + EPSILON)
    q_high = qscale.astype(BF16)
    q_rest = qscale - q_high.astype(F32)
    q_mid = q_rest.astype(BF16)
    q_low = (q_rest - q_mid.astype(F32)).astype(BF16)
    q_parts = jnp.pad(jnp.stack([q_high, q_mid, q_low], axis=1), ((0, 0), (0, LANES - 3)))

    def later(values):
        post = 2.0 * jax.nn.sigmoid(coef_scale[1] * values[4:8] + coef_bias[4:8, None])
        return post, sinkhorn(coef_scale[2] * values[8:] + coef_bias[8:, None])

    (post, mixing), pullback = jax.vjp(later, projection)
    mix_rel = relative(relative(mixing, me, 0), me, 1).reshape(16, count)
    coef = jnp.concatenate([relative(post, me), mix_rel, jnp.zeros((4, count), F32)])
    half = pltpu.VMEM((count, columns), BF16)
    piece = sds((count, columns), BF16)
    moe_out, w_both = lax.optimization_barrier((moe_out, w_both))
    send_c, *grad_mix, cot_sums = call(
        cot_kernel, "cot",
        [sds((slots, wide), BF16), piece, piece, piece, piece, sds((24, count), F32)],
        [coef, combine, moe_out, q_parts, x_all] + y_rel + pick,
        [scratch, scratch, half, half],
        4 * slots * count * columns,
    )
    rows_c = to_experts(send_c)
    h_own, *_ = lax.optimization_barrier((h_own, y_rel[1], y_rel[2], y_rel[3]))
    h_rel = [h_own, shift(h_own, 1), None, shift(h_own, 3)]

    part_both = jnp.dot(rows_u, w_both, preferred_element_type=F32).astype(BF16)
    both = reduce_rows(part_both, me)
    rows_c, both, h_rel[1], h_rel[3] = lax.optimization_barrier((rows_c, both, h_rel[1], h_rel[3]))
    none = jnp.zeros((1,), jnp.int32)
    part_hidden = product(none, [rows_c], w_hidden, "hidden_product")
    quarter = slots // NSTREAM
    hidden = part_hidden.reshape(NSTREAM, quarter, -1)
    hidden = lax.all_to_all(hidden, "stream", split_axis=0, concat_axis=0, tiled=True)
    tail = lax.dynamic_slice(rows_c, (me * quarter, columns), (quarter, LANES))
    d_both = call(hidden_kernel, "hidden", sds(both.shape, BF16), [tail, both, hidden], limit=16)
    d_both = spread(d_both)
    part_du = product(order, d_both, w_both, "input_product")
    back = to_experts(part_du)

    *grad_mix, h_own, _, _, _, _ = lax.optimization_barrier((*grad_mix, h_own, *d_both))
    h_rel[2] = shift(h_own, 2)
    e_rel = [grad_mix[0]] + [shift(grad_mix[(4 - k) % 4], k) for k in range(1, NSTREAM)]
    post_dots = relative(cot_sums[0:4], me)
    mix_dots = relative(cot_sums[4:20].reshape(NSTREAM, NSTREAM, count), me).reshape(16, count)
    cot_sums = small_sum(jnp.concatenate([post_dots, mix_dots, jnp.zeros((4, count), F32)]))
    (d_proj,) = pullback((cot_sums[0:4], cot_sums[4:20].reshape(NSTREAM, NSTREAM, count)))
    early_rscale = jnp.sum(d_proj * projected, axis=0)
    early = rscale[None, :] * d_proj
    small = jnp.concatenate(
        [pre, b_part, projected[0:4], qscale[None], rscale[None], early_rscale[None],
         jnp.broadcast_to(coef_scale[0:1, None], (1, count)),
         lax.dynamic_slice_in_dim(pre, me, 1, 0), jnp.zeros((7, count), F32)]
    )
    back, h_rel[2], *e_rel = lax.optimization_barrier((back, h_rel[2], *e_rel))
    gu_own = call(
        collect_kernel, "collect", sds((count, wide), BF16),
        [back, back_map, norm_gain[None, :], x_all],
        [pltpu.VMEM((count, columns), F32), scratch],
        2 * slots * count * columns, limit=20,
    )
    gu_rel = spread(gu_own)
    four = pltpu.VMEM((NSTREAM, count, columns), BF16)
    grads = call(
        final_kernel, "final", sds((count, NSTREAM * columns), BF16),
        [order, small, early, x_flat] + gu_rel + h_rel + e_rel + tables,
        [
            scratch, pltpu.VMEM((LANES, count), F32), pltpu.VMEM((24, count), F32),
            pltpu.VMEM((24, count), F32), pltpu.VMEM((NSTREAM, count, wide), BF16), four, four, four,
            pltpu.VMEM((NSTREAM, 96, columns), BF16), four,
            dma((2,)), dma((NSTREAM, 8)), dma((NSTREAM,)),
        ],
        2 * count * 96 * NSTREAM * columns, smem=1, anywhere=True,
    )
    return grads.reshape(streams.shape)


def solution(mesh):
    placed = (
        P("expert", "stream", None),
        P("expert", "stream", None),
        P("expert", "stream"),
        P(None, None, "stream"),
        P(),
        P(),
        P("stream"),
        P("expert", None),
        P("expert", None),
        P("stream", "expert"),
        P("stream", "expert"),
        P("expert", "stream"),
    )
    return jax.shard_map(
        shards, mesh=mesh, in_specs=placed, out_specs=P("expert", "stream", None), check_vma=False
    )
```
